32 devices in a mesh: mesh: 16 (over z, x, core), mem: 2 (over y).
Axes of the slice: x: 2, y: 2, z: 4, core: 2. Of those that a mesh axis runs over, the one named last changes fastest.
Arguments:
- perturbations: bfloat16 [3072, 8192], P('mem', 'mesh')
- node_coord: int32 [8192], P('mesh'), may hold values from 0 to 32767, as said below
- threshold_level: int32 [8192], P('mesh'), may hold values from 0 to 4
Outputs:
- band_cov: float32 [8192, 2048], P(('mesh', 'mem'))
The draws below stay inside these ranges and needn't reach their ends.
Inputs may be any that keep to these rules, and one draw needn't show every extreme that they name: node_coord[n] lies in 4 n to 4 n + 3; node 0 has 0 and the last node 32767.
All inputs are finite; a program needn't handle non-finite values.
Results may differ from the reference program's by a relative error of at most 0.0003.
Values may be sent and summed in bfloat16 or wider, within the bound.
No kernel may reach another device: no remote copies, remote signals or barrier semaphores. Data moves between devices by JAX's collectives and lax.ppermute only.
A program may use at most 64 MiB of HBM per device.

```python
import jax
import jax.numpy as jnp
from jax import lax

NB = 512
SHIFTS = 3
FACTORS = 8
NODES = 8192
MEMBERS = 3072
WIDE = 2048
TAPER_HALF = 6144


def draw_perturbations(key, part):
    key_noise = jax.random.fold_in(key, 11)
    key_modes = jax.random.fold_in(key, 12)
    key_load = jax.random.fold_in(key, 13)
    noise = jax.random.normal(key_noise, (MEMBERS, NODES), jnp.float32)
    modes = jax.random.normal(key_modes, (MEMBERS, FACTORS), jnp.float32)
    loads = 0.25 * jax.random.normal(key_load, (FACTORS, NODES), jnp.float32)
    values = noise + jnp.dot(modes, loads, precision=lax.Precision.HIGHEST)
    return values.astype(jnp.bfloat16)


def draw_node_coord(key, part):
    jitter = jax.random.randint(jax.random.fold_in(key, 21), (NODES,), 0, 4)
    jitter = jitter.at[0].set(0).at[NODES - 1].set(3)
    return (4 * jnp.arange(NODES, dtype=jnp.int32) + jitter).astype(jnp.int32)


def set_ends(entries, key, smallest, largest):
    shape = entries.shape
    spot = [jax.random.randint(jax.random.fold_in(key, axis), (), 0, shape[axis]) for axis in range(len(shape))]
    entries = entries.at[tuple(spot)].set(smallest)
    longest = shape.index(max(shape))
    spot[longest] = (spot[longest] + 1) % shape[longest]
    return entries.at[tuple(spot)].set(largest)


def setup_inputs(seed: int = 0) -> dict:
    seeds = jax.random.split(jax.random.key(seed), 4)
    perturbations = draw_perturbations(jax.random.fold_in(seeds[3], 71), 0)
    node_coord = draw_node_coord(jax.random.fold_in(seeds[3], 71), 0)
    threshold_level = set_ends(jax.random.randint(seeds[2], (NODES,), 0, 5), jax.random.fold_in(seeds[2], 1), 0, 4).astype(jnp.int32)
    return {"perturbations": perturbations, "node_coord": node_coord, "threshold_level": threshold_level}


def gc_taper(radius):
    near = -0.25 * radius ** 5 + 0.5 * radius ** 4 + 0.625 * radius ** 3 - (5.0 / 3.0) * radius ** 2 + 1.0
    safe = jnp.maximum(radius, 1.0)
    far = safe ** 5 / 12.0 - 0.5 * safe ** 4 + 0.625 * safe ** 3 + (5.0 / 3.0) * safe ** 2 - 5.0 * safe + 4.0 - 2.0 / (3.0 * safe)
    return jnp.where(radius <= 1.0, near, jnp.where(radius <= 2.0, far, 0.0))


def reference(perturbations, node_coord, threshold_level):
    parts = NODES // NB
    period = 4 * NODES
    whole = perturbations.astype(jnp.float32)

    def one_part(index):
        own = lax.dynamic_slice_in_dim(whole, (index * NB).astype(jnp.int32), NB, 1)
        own_coord = lax.dynamic_slice_in_dim(node_coord, (index * NB).astype(jnp.int32), NB, 0)
        own_level = lax.dynamic_slice_in_dim(threshold_level, (index * NB).astype(jnp.int32), NB, 0)
        level = (0.05 * own_level.astype(jnp.float32))[:, None]
        columns = []
        coords = []
        for step in range(SHIFTS + 1):
            start = (((index + step) % parts) * NB).astype(jnp.int32)
            columns.append(lax.dynamic_slice_in_dim(whole, start, NB, 1))
            coords.append(lax.dynamic_slice_in_dim(node_coord, start, NB, 0))
        columns = jnp.concatenate(columns, axis=1)
        coords = jnp.concatenate(coords, axis=0)
        raw = lax.dot_general(own, columns, (((0,), (0,)), ((), ())), precision=lax.Precision.HIGHEST, preferred_element_type=jnp.float32)
        cov = raw / jnp.float32(MEMBERS - 1)
        gap = jnp.mod(coords[None, :] - own_coord[:, None], period)
        dist = jnp.minimum(gap, period - gap).astype(jnp.float32)
        taper = gc_taper(dist / jnp.float32(TAPER_HALF))
        tapered = taper * cov
        return tapered - jnp.clip(tapered, -level, level)

    blocks = lax.map(one_part, jnp.arange(parts, dtype=jnp.int32))
    return blocks.reshape(NODES, WIDE)
```

```python
import functools

import jax
import jax.numpy as jnp
from jax import lax
from jax.experimental import pallas as pl
from jax.experimental.pallas import tpu as pltpu
from jax.sharding import PartitionSpec as P

PAD = 16
CHUNK = 128
PARAMS = pltpu.CompilerParams(vmem_limit_bytes=32 * 1024 * 1024)


def gc_taper(r):
    near = 1.0 + r * r * (-5.0 / 3.0 + r * (0.625 + r * (0.5 - 0.25 * r)))
    s = jnp.maximum(r, 1.0)
    far = 4.0 - 5.0 * s + s * s * (5.0 / 3.0 + s * (0.625 + s * (s * (1.0 / 12.0) - 0.5))) - (2.0 / 3.0) / s
    return jnp.where(r <= 1.0, near, jnp.where(r <= 2.0, far, 0.0))


def own_kernel(place, x, lt, *outs, owned, split):
    members, width = x.shape
    groups = width // owned
    for part in range(groups):
        if split:
            start = pl.multiple_of(lax.rem(place[0] + 1 + part, groups) * owned, owned)
        else:
            start = part * owned
        rows = x[:, pl.ds(start, owned)].T
        lt[part * owned : (part + 1) * owned, :] = rows
        tile = jnp.dot(rows, x[...], preferred_element_type=jnp.float32)
        if split:
            outs[part][...] = tile
        else:
            outs[0][part * owned : (part + 1) * owned, :] = tile


def own_tile(place, x, owned, split):
    members, width = x.shape
    rows = [owned] * (width // owned) if split else [width]
    return pl.pallas_call(
        functools.partial(own_kernel, owned=owned, split=split),
        out_shape=[jax.ShapeDtypeStruct((width, members), x.dtype)]
        + [jax.ShapeDtypeStruct((r, width), jnp.float32) for r in rows],
        in_specs=[pl.BlockSpec(memory_space=pltpu.SMEM), pl.BlockSpec(memory_space=pltpu.VMEM)],
        out_specs=[pl.BlockSpec(memory_space=pltpu.VMEM)] * (1 + len(rows)),
        compiler_params=PARAMS,
        cost_estimate=pl.CostEstimate(flops=2 * members * width * width, bytes_accessed=5 << 20, transcendentals=0),
        name="own_tile",
    )(place, x)


def panel_kernel(place, lt, *refs, picks, count, rows):
    panels, cols, outs = refs[:count], refs[count], refs[count + 1 :]
    members = lt.shape[1]

    def run(which):
        at = 0
        for slot, index in enumerate(which):
            panel = panels[index]
            wide = panel.shape[1]
            first = 0
            for out, r in zip(outs, rows):
                out[:, at : at + wide] = jnp.dot(
                    lt[first : first + r, :], panel[:members, :], preferred_element_type=jnp.float32
                )
                first += r
            node = place[2 + slot] + lax.broadcasted_iota(jnp.int32, (8, wide), 1)
            jitter = panel[members : members + PAD, :].astype(jnp.float32)[:8]
            cols[:, at : at + wide] = (4 * node).astype(jnp.float32) + jitter
            at += wide

    if len(picks) == 1:
        run(picks[0])
    else:
        for value, which in enumerate(picks):
            pl.when(place[1] == value)(functools.partial(run, which))


def panel_tile(place, lt, panels, picks, rows):
    wide = sum(panels[i].shape[1] for i in picks[0])
    width, members = lt.shape
    return pl.pallas_call(
        functools.partial(panel_kernel, picks=picks, count=len(panels), rows=rows),
        out_shape=[jax.ShapeDtypeStruct((8, wide), jnp.float32)]
        + [jax.ShapeDtypeStruct((r, wide), jnp.float32) for r in rows],
        in_specs=[pl.BlockSpec(memory_space=pltpu.SMEM)]
        + [pl.BlockSpec(memory_space=pltpu.VMEM)] * (1 + len(panels)),
        out_specs=[pl.BlockSpec(memory_space=pltpu.VMEM)] * (1 + len(rows)),
        compiler_params=PARAMS,
        cost_estimate=pl.CostEstimate(flops=2 * members * width * wide, bytes_accessed=3 << 20, transcendentals=0),
        name="panel_tile",
    )(place, lt, *panels)


def finish_kernel(block, row_coord, row_level, cols, *refs, period, half, members):
    parts, out = refs[:-1], refs[-1]
    raw = parts[0][...]
    for extra in parts[1:-1]:
        raw = raw + extra[...]
    cov = raw * jnp.float32(1.0 / (members - 1))
    wide = out.shape[1]
    level = row_level[...]
    coord = row_coord[...]
    if wide != level.shape[1]:
        level = jnp.concatenate([level] * (wide // level.shape[1]), axis=1)
        coord = jnp.concatenate([coord] * (wide // coord.shape[1]), axis=1)
    gap = jnp.abs(cols[0:1, :] - coord)
    dist = jnp.minimum(gap, period - gap)
    c = gc_taper(dist * jnp.float32(1.0 / half)) * cov
    out[...] = c - jnp.clip(c, -level, level)


def finish(block, row_coord, row_level, cols, parts, out, shape, count, period, half, members):
    owned, wide = parts[0].shape
    piece = wide // count
    first = out is None
    specs = (
        [pl.BlockSpec((owned, CHUNK), lambda i, b: (0, 0))] * 2
        + [pl.BlockSpec((8, piece), lambda i, b: (0, i))]
        + [pl.BlockSpec((owned, piece), lambda i, b: (0, i))] * len(parts)
    )
    operands = [block, row_coord, row_level, cols, *parts]
    if first:
        kernel = lambda b, rc, rl, co, *refs: finish_kernel(
            b, rc, rl, co, *refs[:-1], None, refs[-1], period=period, half=half, members=members
        )
        aliases = {}
    else:
        specs.append(pl.BlockSpec(memory_space=pl.ANY))
        operands.append(out)
        kernel = functools.partial(finish_kernel, period=period, half=half, members=members)
        aliases = {len(operands) - 1: 0}
    return pl.pallas_call(
        kernel,
        out_shape=jax.ShapeDtypeStruct(shape, jnp.float32),
        grid_spec=pltpu.PrefetchScalarGridSpec(
            num_scalar_prefetch=1,
            grid=(count,),
            in_specs=specs,
            out_specs=pl.BlockSpec((owned, piece), lambda i, b: (0, b[i])),
        ),
        input_output_aliases=aliases,
        compiler_params=PARAMS,
        cost_estimate=pl.CostEstimate(flops=20 * owned * wide, bytes_accessed=16 * owned * wide, transcendentals=0),
        name="finish",
    )(*operands)


def per_device(perturbations, node_coord, threshold_level):
    members, width = perturbations.shape
    groups = lax.axis_size("mem")
    count = lax.axis_size("mesh")
    nodes = width * count
    period = 4.0 * nodes
    half = 12 * width
    owned = width // groups
    everyone = members * groups
    split = groups == 2
    rows = [owned] * groups if split else [width]
    shape = (owned, 4 * width)
    mem = lax.axis_index("mem")
    me = lax.axis_index("mesh")
    odd = me % 2
    cross = (me // 2) % 2

    def permute(array, pairs):
        return lax.ppermute(array, "mesh", pairs)

    everywhere = range(count)
    swap_x = [(p, p ^ 2) for p in everywhere]
    relay = [(p, (p - 4) % count) if p % 4 >= 2 else (p, p ^ 1) for p in everywhere]
    far_siblings = [(p, p ^ 1) for p in everywhere if p % 4 >= 2]
    back_two = [(p, (p - 2) % count) for p in everywhere]
    siblings = [(p, p ^ 1) for p in everywhere]
    extra_pairs = [(p, p - 1) if p % 2 else (p, (p - 3) % count) for p in everywhere]

    def reduced(parts):
        if split:
            return [parts[1], lax.ppermute(parts[0], "mem", [(0, 1), (1, 0)])]
        return [lax.psum_scatter(parts[0], "mem", scatter_dimension=0, tiled=True)]

    jitter = (node_coord - 4 * (me * width + jnp.arange(width, dtype=jnp.int32))).astype(perturbations.dtype)
    panel = jnp.concatenate([perturbations, jnp.broadcast_to(jitter[None, :], (PAD, width))], axis=0)
    chunks = [panel[:, i * CHUNK : (i + 1) * CHUNK] for i in range(width // CHUNK)]
    relayed = len(chunks) // 2

    first_row = mem * owned
    row_coord = lax.dynamic_slice_in_dim(node_coord, first_row, owned, 0).astype(jnp.float32)
    row_level = 0.05 * lax.dynamic_slice_in_dim(threshold_level, first_row, owned, 0).astype(jnp.float32)
    row_coord = jnp.broadcast_to(row_coord[:, None], (owned, CHUNK))
    row_level = jnp.broadcast_to(row_level[:, None], (owned, CHUNK))
    own_cols = jnp.broadcast_to(node_coord.astype(jnp.float32)[None, :], (8, width))

    def done(out, blocks, cols, parts, pieces):
        block = jnp.stack([jnp.asarray(b, jnp.int32) for b in blocks])
        return finish(block, row_coord, row_level, cols, parts, out, shape, pieces, period, half, everyone)

    def place(*starts):
        return jnp.stack([mem, cross] + [jnp.asarray(s, jnp.int32) for s in starts]).astype(jnp.int32)

    arrived = [permute(c, swap_x) for c in chunks[:relayed]]
    extra = permute(panel, extra_pairs)
    arrived += [permute(c, back_two) for c in chunks[relayed:]]

    lt, *own = own_tile(place(), perturbations, owned, split)
    own = reduced(own)

    passed = [permute(a, relay) for a in arrived[:relayed]]
    passed_on = [permute(a, far_siblings) for a in passed]
    others = [permute(a, siblings) for a in arrived[relayed:]]

    def first_node(step):
        return ((me + step) % count) * width

    extra_step = 1 + 2 * odd
    other_step = 3 - 2 * odd
    extra_cols, *extra_parts = panel_tile(place(first_node(extra_step)), lt, [extra], [[0]], rows)
    extra_parts = reduced(extra_parts)

    per_panel = width // CHUNK
    pieces = []
    for i in range(per_panel):
        at = place(first_node(2) + i * CHUNK, first_node(other_step) + i * CHUNK)
        if i < relayed:
            panels, picks = [arrived[i], passed[i], passed_on[i]], [[0, 1], [1, 2]]
        else:
            panels, picks = [arrived[i], others[i - relayed]], [[0, 1]]
        cols, *parts = panel_tile(at, lt, panels, picks, rows)
        pieces.append((cols, reduced(parts)))

    out = done(None, [0], own_cols, own, 1)
    out = done(out, [extra_step], extra_cols, extra_parts, 1)
    for i, (cols, parts) in enumerate(pieces):
        out = done(out, [2 * per_panel + i, other_step * per_panel + i], cols, parts, 2)
    return out


def solution(mesh):
    in_specs = (P("mem", "mesh"), P("mesh"), P("mesh"))
    out_specs = P(("mesh", "mem"), None)
    return jax.shard_map(
        per_device, mesh=mesh, in_specs=in_specs, out_specs=out_specs, check_vma=False
    )
```

```python
import functools

import jax
import jax.numpy as jnp
from jax import lax
from jax.experimental import pallas as pl
from jax.experimental.pallas import tpu as pltpu
from jax.sharding import PartitionSpec as P

PAD = 16
CHUNK = 128
PARAMS = pltpu.CompilerParams(vmem_limit_bytes=32 * 1024 * 1024)
VMEM = pl.BlockSpec(memory_space=pltpu.VMEM)
F32 = jnp.float32


def after(value, *tokens):
    return lax.optimization_barrier((value, *tokens))[0]


def call(kernel, outs, *operands, name, flops=0):
    size = sum(o.size * o.dtype.itemsize for o in (*outs, *operands))
    return pl.pallas_call(
        kernel,
        out_shape=outs,
        in_specs=[VMEM] * len(operands),
        out_specs=[VMEM] * len(outs),
        compiler_params=PARAMS,
        cost_estimate=pl.CostEstimate(flops=1, bytes_accessed=1, transcendentals=0),
        name=name,
    )(*operands)


def gc_taper(r):
    near = 1.0 + r * r * (-5.0 / 3.0 + r * (0.625 + r * (0.5 - 0.25 * r)))
    s = jnp.maximum(r, 1.0)
    far = 4.0 - 5.0 * s + s * s * (5.0 / 3.0 + s * (0.625 + s * (s * (1.0 / 12.0) - 0.5))) - (2.0 / 3.0) / s
    return jnp.where(r <= 1.0, near, jnp.where(r <= 2.0, far, 0.0))


def prepare_kernel(x, coord, low, high, *chunks):
    members, width = x.shape
    first = 4 * width * lax.axis_index("mesh")
    jitter = coord[...] - first - 4 * lax.broadcasted_iota(jnp.int32, (1, width), 1)
    pad = jnp.broadcast_to(jitter.astype(F32), (PAD, width)).astype(x.dtype)
    for i, chunk in enumerate(chunks):
        span = slice(i * CHUNK, (i + 1) * CHUNK)
        chunk[:members, :] = x[:, span]
        chunk[members:, :] = pad[:, span]
    half = width // 2
    for part, span in ((low, slice(0, half)), (high, slice(half, width))):
        part[:members, :] = x[:, span]
        part[members:, :] = pad[:, span]


def own_kernel(x, coord, level, lt, row_coord, row_level, *outs, owned, split):
    members, width = x.shape
    groups = width // owned
    mem = lax.axis_index("mem")
    for part in range(groups):
        if split:
            start = pl.multiple_of(lax.rem(mem + 1 + part, groups) * owned, owned)
        else:
            start = part * owned
        lt[part * owned : (part + 1) * owned, :] = x[:, pl.ds(start, owned)].T
    tile = jnp.dot(lt[...], x[...], preferred_element_type=F32)
    store_rows(tile, outs, 0)
    rows = jnp.concatenate(
        [jnp.broadcast_to(coord[...], (CHUNK, width)), jnp.broadcast_to(level[...], (CHUNK, width))], axis=0
    )
    rows = rows.astype(F32)
    for part in range(groups):

        @pl.when(mem == part)
        def _():
            span = slice(part * owned, (part + 1) * owned)
            row_coord[...] = rows[:CHUNK, span].T
            row_level[...] = 0.05 * rows[CHUNK:, span].T


def store_rows(tile, outs, at):
    first = 0
    for out in outs:
        out[:, at : at + tile.shape[1]] = tile[first : first + out.shape[0]]
        first += out.shape[0]


def own_tile(x, coord, level, owned, rows):
    members, width = x.shape
    return call(
        functools.partial(own_kernel, owned=owned, split=len(rows) > 1),
        [jax.ShapeDtypeStruct((width, members), x.dtype)]
        + [jax.ShapeDtypeStruct((owned, CHUNK), F32)] * 2
        + [jax.ShapeDtypeStruct((r, width), F32) for r in rows],
        x,
        coord,
        level,
        name="own_tile",
        flops=2 * members * width * width,
    )


def panel_kernel(lt, *refs, picks, count, rows):
    panels, cols, outs = refs[:count], refs[count], refs[count + 1 :]
    members = lt.shape[1]

    def run(which):
        chosen = [panels[i] for i in which]
        at = 0
        for panel in chosen:
            wide = panel.shape[1]
            cols[:, at : at + wide] = panel[members:, :].astype(F32)[:8]
            at += wide
        block = jnp.concatenate([panel[:members, :] for panel in chosen], axis=1)
        store_rows(jnp.dot(lt[...], block, preferred_element_type=F32), outs, 0)

    if len(picks) == 1:
        run(picks[0])
    else:
        cross = lax.rem(lax.axis_index("mesh") // 2, 2)
        for value, which in enumerate(picks):
            pl.when(cross == value)(functools.partial(run, which))


def panel_tile(lt, panels, picks, rows):
    wide = sum(panels[i].shape[1] for i in picks[0])
    width, members = lt.shape
    return call(
        functools.partial(panel_kernel, picks=picks, count=len(panels), rows=rows),
        [jax.ShapeDtypeStruct((8, wide), F32)] + [jax.ShapeDtypeStruct((r, wide), F32) for r in rows],
        lt,
        *panels,
        name="panel_tile",
        flops=2 * members * width * wide,
    )


def finish_kernel(row_coord, row_level, *refs, plan, period, width, members, first):
    operands = sum(1 + n for n, _ in plan)
    out, scratch, sems = refs[-3], refs[-2], refs[-1]
    me = lax.axis_index("mesh")
    count = lax.axis_size("mesh")
    odd = lax.rem(me, 2)
    coord, level = row_coord[...], row_level[...]
    steps = {"own": 0, "two": 2, "extra": 1 + 2 * odd, "other": 3 - 2 * odd}
    copies = []
    at, slot = 0, 0
    for n, spans in plan:
        cols, parts = refs[at], refs[at + 1 : at + 1 + n]
        at += 1 + n
        for offset, wide, kind, inside in spans:
            step = steps[kind]
            base = (4 * (lax.rem(me + step, count) * width + inside)).astype(F32)
            for piece in range(0, wide, CHUNK):
                span = slice(offset + piece, offset + piece + CHUNK)
                raw = parts[0][:, span]
                for part in parts[1:]:
                    raw = raw + part[:, span]
                place = 4 * (piece + lax.broadcasted_iota(jnp.int32, (1, CHUNK), 1))
                column = cols[0:1, span] + (base + place.astype(F32))
                gap = jnp.abs(column - coord)
                dist = jnp.minimum(gap, period - gap)
                c = gc_taper(dist * (1.0 / (12 * width))) * (raw * (1.0 / (members - 1)))
                scratch[:, slot * CHUNK : (slot + 1) * CHUNK] = c - jnp.clip(c, -level, level)
                slot += 1
            begin = (slot * CHUNK) - wide
            target = pl.multiple_of(step * width + inside, CHUNK)
            copy = pltpu.make_async_copy(
                scratch.at[:, begin : begin + wide], out.at[:, pl.ds(target, wide)], sems.at[len(copies)]
            )
            copy.start()
            copies.append(copy)
    for copy in copies:
        copy.wait()


def finish(row_coord, row_level, groups, out, shape, period, width, members):
    operands = [row_coord, row_level]
    plan, wide, copies = [], 0, 0
    for cols, parts, spans in groups:
        operands += [cols, *parts]
        plan.append((len(parts), spans))
        wide += sum(s[1] for s in spans)
        copies += len(spans)
    specs = [VMEM] * len(operands)
    aliases = {}
    if out is not None:
        aliases = {len(operands): 0}
        operands.append(out)
        specs.append(pl.BlockSpec(memory_space=pl.ANY))
    owned = shape[0]
    return pl.pallas_call(
        functools.partial(
            finish_kernel, plan=plan, period=period, width=width, members=members, first=out is None
        ),
        out_shape=jax.ShapeDtypeStruct(shape, F32),
        in_specs=specs,
        out_specs=pl.BlockSpec(memory_space=pl.ANY),
        scratch_shapes=[pltpu.VMEM((owned, wide), F32), pltpu.SemaphoreType.DMA((copies,))],
        input_output_aliases=aliases,
        compiler_params=PARAMS,
        cost_estimate=pl.CostEstimate(flops=1, bytes_accessed=1, transcendentals=0),
        name="finish",
    )(*operands)


def per_device(perturbations, node_coord, threshold_level):
    members, width = perturbations.shape
    groups = lax.axis_size("mem")
    count = lax.axis_size("mesh")
    period = 4.0 * width * count
    owned = width // groups
    everyone = members * groups
    split = groups == 2
    rows = [owned] * groups if split else [width]
    shape = (owned, 4 * width)
    coord = node_coord.reshape(1, width)
    levels = threshold_level.reshape(1, width)

    def permute(array, pairs):
        return lax.ppermute(array, "mesh", pairs)

    everywhere = range(count)
    swap_x = [(p, p ^ 2) for p in everywhere]
    relay = [(p, (p - 4) % count) if p % 4 >= 2 else (p, p ^ 1) for p in everywhere]
    far_siblings = [(p, p ^ 1) for p in everywhere if p % 4 >= 2]
    back_two = [(p, (p - 2) % count) for p in everywhere]
    siblings = [(p, p ^ 1) for p in everywhere]
    extra_pairs = [(p, p - 1) if p % 2 else (p, (p - 3) % count) for p in everywhere]

    def reduced(parts):
        if split:
            return [parts[1], lax.ppermute(parts[0], "mem", [(0, 1), (1, 0)])]
        return [lax.psum_scatter(parts[0], "mem", scatter_dimension=0, tiled=True)]

    pieces = width // CHUNK
    relayed = pieces // 2
    low, high, *chunks = call(
        prepare_kernel,
        [jax.ShapeDtypeStruct((members + PAD, width // 2), perturbations.dtype)] * 2
        + [jax.ShapeDtypeStruct((members + PAD, CHUNK), perturbations.dtype)] * pieces,
        perturbations,
        coord,
        name="prepare",
    )
    lt, row_coord, row_level, *own = own_tile(after(perturbations, low), coord, levels, owned, rows)
    own_parts = reduced(own)
    own_done = own_parts[-1]
    own_cols = jnp.concatenate([low[members : members + 8], high[members : members + 8]], axis=1).astype(F32)

    def finished(out, groups):
        return finish(row_coord, row_level, groups, out, shape, period, width, everyone)

    extra = [permute(a, extra_pairs) for a in (low, high)]
    first = [permute(chunks[0], swap_x)]
    first.append(permute(after(chunks[1], first[0], lt), swap_x))
    straight = [permute(after(chunks[2], first[1], own_done), back_two)]
    straight.append(permute(after(chunks[3], straight[0]), back_two))
    passed = [permute(after(a, first[1], own_done), relay) for a in first]

    extra_cols, *extra_parts = panel_tile(after(lt, own_done), extra, [[0, 1]], rows)
    extra_parts = reduced(extra_parts)
    token = extra_parts[-1]

    out = None
    groups = [
        (own_cols, own_parts, [(0, width, "own", 0)]),
        (extra_cols, extra_parts, [(0, width, "extra", 0)]),
    ]
    for i in range(2):
        other = permute(after(straight[i], passed[i], *([cols] if i else [])), siblings)
        far = permute(after(passed[i], *([other, token] if i else [])), far_siblings)
        panels = [first[i], passed[i], far, straight[i], other]
        cols, *parts = panel_tile(after(lt, token), panels, [[0, 1, 3, 4], [1, 2, 3, 4]], rows)
        out = finished(out, [(after(groups[0][0], cols), *groups[0][1:])] + groups[1:])
        spans = []
        for at, index in ((0, i), (2 * CHUNK, i + 2)):
            spans += [(at, CHUNK, "two", index * CHUNK), (at + CHUNK, CHUNK, "other", index * CHUNK)]
        groups = [(cols, reduced(parts), spans)]
        token = groups[0][1][-1]
    return finished(out, groups)


def solution(mesh):
    in_specs = (P("mem", "mesh"), P("mesh"), P("mesh"))
    out_specs = P(("mesh", "mem"), None)
    return jax.shard_map(
        per_device, mesh=mesh, in_specs=in_specs, out_specs=out_specs, check_vma=False
    )
```

```python
import functools

import jax
import jax.numpy as jnp
from jax import lax
from jax.experimental import pallas as pl
from jax.experimental.pallas import tpu as pltpu
from jax.sharding import PartitionSpec as P

PAD = 16
STEPS = 32766.0
CHUNK = 128
PARAMS = pltpu.CompilerParams(vmem_limit_bytes=32 * 1024 * 1024)
VMEM = pl.BlockSpec(memory_space=pltpu.VMEM)
F32 = jnp.float32


def after(value, *tokens):
    return lax.optimization_barrier((value, *tokens))[0]


def call(kernel, outs, *operands, name, flops=0):
    size = sum(o.size * o.dtype.itemsize for o in (*outs, *operands))
    return pl.pallas_call(
        kernel,
        out_shape=outs,
        in_specs=[VMEM] * len(operands),
        out_specs=[VMEM] * len(outs),
        compiler_params=PARAMS,
        cost_estimate=pl.CostEstimate(flops=1, bytes_accessed=1, transcendentals=0),
        name=name,
    )(*operands)


def gc_taper(r):
    near = 1.0 + r * r * (-5.0 / 3.0 + r * (0.625 + r * (0.5 - 0.25 * r)))
    s = jnp.maximum(r, 1.0)
    far = 4.0 - 5.0 * s + s * s * (5.0 / 3.0 + s * (0.625 + s * (s * (1.0 / 12.0) - 0.5))) - (2.0 / 3.0) / s
    return jnp.where(r <= 1.0, near, jnp.where(r <= 2.0, far, 0.0))


def prepare_kernel(x, coord, low, high):
    members, width = x.shape
    first = 4 * width * lax.axis_index("mesh")
    jitter = coord[...] - first - 4 * lax.broadcasted_iota(jnp.int32, (1, width), 1)
    pad = jnp.broadcast_to(jitter.astype(F32), (PAD, width)).astype(x.dtype)
    half = width // 2
    for part, span in ((low, slice(0, half)), (high, slice(half, width))):
        part[:members, :] = x[:, span]
        part[members:, :] = pad[:, span]


def own_kernel(x, coord, level, lt, row_coord, row_level, *outs, owned, split):
    members, width = x.shape
    groups = width // owned
    mem = lax.axis_index("mem")
    for part in range(groups):
        if split:
            start = pl.multiple_of(lax.rem(mem + 1 + part, groups) * owned, owned)
        else:
            start = part * owned
        lt[part * owned : (part + 1) * owned, :] = x[:, pl.ds(start, owned)].T
    tile = jnp.dot(lt[...], x[...], preferred_element_type=F32)
    store_rows(tile, outs, 0)
    rows = jnp.concatenate(
        [jnp.broadcast_to(coord[...], (CHUNK, width)), jnp.broadcast_to(level[...], (CHUNK, width))], axis=0
    )
    rows = rows.astype(F32)
    for part in range(groups):

        @pl.when(mem == part)
        def _():
            span = slice(part * owned, (part + 1) * owned)
            row_coord[...] = rows[:CHUNK, span].T
            row_level[...] = 0.05 * rows[CHUNK:, span].T


def store_rows(tile, outs, at):
    first = 0
    for out in outs:
        out[:, at : at + tile.shape[1]] = tile[first : first + out.shape[0]]
        first += out.shape[0]


def own_tile(x, coord, level, owned, rows):
    members, width = x.shape
    return call(
        functools.partial(own_kernel, owned=owned, split=len(rows) > 1),
        [jax.ShapeDtypeStruct((width, members), x.dtype)]
        + [jax.ShapeDtypeStruct((owned, CHUNK), F32)] * 2
        + [jax.ShapeDtypeStruct((r, width), F32) for r in rows],
        x,
        coord,
        level,
        name="own_tile",
        flops=2 * members * width * width,
    )


def narrowed(block):
    top = jnp.maximum(jnp.max(jnp.abs(block), axis=0, keepdims=True), 2.0**-126)
    power = jnp.ceil(8.0 * jnp.log2(top) + 0.01)
    steps = jnp.round(block * jnp.exp2(-0.125 * power) * STEPS)
    return steps.astype(jnp.int32), power.astype(jnp.int32)


def widened(steps, power):
    return (steps.astype(F32) * jnp.exp2(0.125 * power.astype(F32) - 16.0)) * (65536.0 / STEPS)


def pack(tile, packed):
    rows = tile.shape[0]
    for at in range(0, tile.shape[1] // 2, CHUNK):
        span = slice(at, at + CHUNK)
        high, high_power = narrowed(tile[:, 2 * at : 2 * at + CHUNK])
        low, low_power = narrowed(tile[:, 2 * at + CHUNK : 2 * at + 2 * CHUNK])
        packed[:rows, span] = (high << 16) | (low & 0xFFFF)
        packed[rows : rows + 4, span] = jnp.broadcast_to(high_power, (4, CHUNK))
        packed[rows + 4 :, span] = jnp.broadcast_to(low_power, (4, CHUNK))


def unpack(packed, block, rows):
    span = slice((block // 2) * CHUNK, (block // 2 + 1) * CHUNK)
    words = packed[:rows, span]
    if block % 2 == 0:
        return widened(words >> 16, packed[rows : rows + 1, span])
    return widened((words << 16) >> 16, packed[rows + 4 : rows + 5, span])


def panel_kernel(lt, *refs, picks, count, rows):
    panels, cols, outs = refs[:count], refs[count], refs[count + 1 :]
    members = lt.shape[1]

    def run(which):
        chosen = [panels[i] for i in which]
        at = 0
        for panel in chosen:
            wide = panel.shape[1]
            cols[:, at : at + wide] = panel[members:, :].astype(F32)[:8]
            at += wide
        block = jnp.concatenate([panel[:members, :] for panel in chosen], axis=1)
        tile = jnp.dot(lt[...], block, preferred_element_type=F32)
        if len(rows) > 1:
            pack(tile[: rows[0]], outs[0])
            outs[1][...] = tile[rows[0] :]
        else:
            outs[0][...] = tile

    if len(picks) == 1:
        run(picks[0])
    else:
        cross = lax.rem(lax.axis_index("mesh") // 2, 2)
        for value, which in enumerate(picks):
            pl.when(cross == value)(functools.partial(run, which))


def panel_tile(lt, panels, picks, rows):
    wide = sum(panels[i].shape[1] for i in picks[0])
    width, members = lt.shape
    return call(
        functools.partial(panel_kernel, picks=picks, count=len(panels), rows=rows),
        [jax.ShapeDtypeStruct((8, wide), F32)]
        + ([jax.ShapeDtypeStruct((rows[0] + 8, wide // 2), jnp.int32)] if len(rows) > 1 else [])
        + [jax.ShapeDtypeStruct((rows[-1], wide), F32)],
        lt,
        *panels,
        name="panel_tile",
        flops=2 * members * width * wide,
    )


def finish_kernel(row_coord, row_level, *refs, plan, period, width, members, first):
    operands = sum(1 + n for n, _ in plan)
    out, scratch, sems = refs[-3], refs[-2], refs[-1]
    me = lax.axis_index("mesh")
    count = lax.axis_size("mesh")
    odd = lax.rem(me, 2)
    coord, level = row_coord[...], row_level[...]
    steps = {"own": 0, "two": 2, "extra": 1 + 2 * odd, "other": 3 - 2 * odd}
    copies = []
    at, slot = 0, 0
    for n, spans in plan:
        cols, parts = refs[at], refs[at + 1 : at + 1 + n]
        at += 1 + n
        for offset, wide, kind, inside in spans:
            step = steps[kind]
            base = (4 * (lax.rem(me + step, count) * width + inside)).astype(F32)
            for piece in range(0, wide, CHUNK):
                span = slice(offset + piece, offset + piece + CHUNK)
                raw = parts[0][:, span]
                for part in parts[1:]:
                    if part.dtype == jnp.int32:
                        raw = raw + unpack(part, span.start // CHUNK, raw.shape[0])
                    else:
                        raw = raw + part[:, span]
                place = 4 * (piece + lax.broadcasted_iota(jnp.int32, (1, CHUNK), 1))
                column = cols[0:1, span] + (base + place.astype(F32))
                gap = jnp.abs(column - coord)
                dist = jnp.minimum(gap, period - gap)
                c = gc_taper(dist * (1.0 / (12 * width))) * (raw * (1.0 / (members - 1)))
                scratch[:, slot * CHUNK : (slot + 1) * CHUNK] = c - jnp.clip(c, -level, level)
                slot += 1
            begin = (slot * CHUNK) - wide
            target = pl.multiple_of(step * width + inside, CHUNK)
            copy = pltpu.make_async_copy(
                scratch.at[:, begin : begin + wide], out.at[:, pl.ds(target, wide)], sems.at[len(copies)]
            )
            copy.start()
            copies.append(copy)
    for copy in copies:
        copy.wait()


def finish(row_coord, row_level, groups, out, shape, period, width, members):
    operands = [row_coord, row_level]
    plan, wide, copies = [], 0, 0
    for cols, parts, spans in groups:
        operands += [cols, *parts]
        plan.append((len(parts), spans))
        wide += sum(s[1] for s in spans)
        copies += len(spans)
    specs = [VMEM] * len(operands)
    aliases = {}
    if out is not None:
        aliases = {len(operands): 0}
        operands.append(out)
        specs.append(pl.BlockSpec(memory_space=pl.ANY))
    owned = shape[0]
    return pl.pallas_call(
        functools.partial(
            finish_kernel, plan=plan, period=period, width=width, members=members, first=out is None
        ),
        out_shape=jax.ShapeDtypeStruct(shape, F32),
        in_specs=specs,
        out_specs=pl.BlockSpec(memory_space=pl.ANY),
        scratch_shapes=[pltpu.VMEM((owned, wide), F32), pltpu.SemaphoreType.DMA((copies,))],
        input_output_aliases=aliases,
        compiler_params=PARAMS,
        cost_estimate=pl.CostEstimate(flops=1, bytes_accessed=1, transcendentals=0),
        name="finish",
    )(*operands)


def per_device(perturbations, node_coord, threshold_level):
    members, width = perturbations.shape
    groups = lax.axis_size("mem")
    count = lax.axis_size("mesh")
    period = 4.0 * width * count
    owned = width // groups
    everyone = members * groups
    split = groups == 2
    rows = [owned] * groups if split else [width]
    shape = (owned, 4 * width)
    coord = node_coord.reshape(1, width)
    levels = threshold_level.reshape(1, width)

    def permute(array, pairs):
        return lax.ppermute(array, "mesh", pairs)

    everywhere = range(count)
    swap_x = [(p, p ^ 2) for p in everywhere]
    relay = [(p, (p - 4) % count) if p % 4 >= 2 else (p, p ^ 1) for p in everywhere]
    far_siblings = [(p, p ^ 1) for p in everywhere if p % 4 >= 2]
    back_two = [(p, (p - 2) % count) for p in everywhere]
    siblings = [(p, p ^ 1) for p in everywhere]
    extra_pairs = [(p, p - 1) if p % 2 else (p, (p - 3) % count) for p in everywhere]

    def reduced(parts):
        if split:
            return [parts[1], lax.ppermute(parts[0], "mem", [(0, 1), (1, 0)])]
        return [lax.psum_scatter(parts[0], "mem", scatter_dimension=0, tiled=True)]

    half = width // 2
    low, high = call(
        prepare_kernel,
        [jax.ShapeDtypeStruct((members + PAD, half), perturbations.dtype)] * 2,
        perturbations,
        coord,
        name="prepare",
    )
    lt, row_coord, row_level, *own = own_tile(after(perturbations, low), coord, levels, owned, rows)
    own_parts = reduced(own)
    own_cols = jnp.concatenate([low[members : members + 8], high[members : members + 8]], axis=1).astype(F32)

    first = permute(low, swap_x)
    extra = [permute(a, extra_pairs) for a in (low, high)]
    straight = permute(high, back_two)
    passed = permute(first, relay)

    def tile(panels, picks, *tokens):
        cols, *parts = panel_tile(after(lt, *tokens), panels, picks, rows)
        return cols, reduced(parts)

    def finished(out, token, *groups):
        groups = [(after(groups[0][0], token), *groups[0][1:])] + list(groups[1:])
        return finish(row_coord, row_level, groups, out, shape, period, width, everyone)

    extra_cols, extra_parts = tile(extra, [[0, 1]], own_parts[-1])
    other = permute(after(straight, extra_parts[-1]), siblings)
    two_cols, two_parts = tile([straight], [[0]], extra_cols)
    far = permute(after(passed, two_parts[-1]), far_siblings)
    other_cols, other_parts = tile([other], [[0]], two_cols)
    out = finished(
        None,
        other_cols,
        (own_cols, own_parts, [(0, width, "own", 0)]),
        (extra_cols, extra_parts, [(0, width, "extra", 0)]),
    )
    low_cols, low_parts = tile([first, passed, far], [[0, 1], [1, 2]], out, other_parts[-1])
    out = finished(
        out,
        low_cols,
        (two_cols, two_parts, [(0, half, "two", half)]),
        (other_cols, other_parts, [(0, half, "other", half)]),
    )
    return finished(
        out,
        low_cols,
        (low_cols, low_parts, [(0, half, "two", 0), (half, half, "other", 0)]),
    )


def solution(mesh):
    in_specs = (P("mem", "mesh"), P("mesh"), P("mesh"))
    out_specs = P(("mesh", "mem"), None)
    return jax.shard_map(
        per_device, mesh=mesh, in_specs=in_specs, out_specs=out_specs, check_vma=False
    )
```

```python
import functools

import jax
import jax.numpy as jnp
from jax import lax
from jax.experimental import pallas as pl
from jax.experimental.pallas import tpu as pltpu
from jax.sharding import PartitionSpec as P

PAD = 16
STEPS = 32766.0
CHUNK = 128
PARAMS = pltpu.CompilerParams(vmem_limit_bytes=32 * 1024 * 1024)
VMEM = pl.BlockSpec(memory_space=pltpu.VMEM)
F32 = jnp.float32


def after(value, *tokens):
    return lax.optimization_barrier((value, *tokens))[0]


def call(kernel, outs, *operands, name, flops=0):
    size = sum(o.size * o.dtype.itemsize for o in (*outs, *operands))
    return pl.pallas_call(
        kernel,
        out_shape=outs,
        in_specs=[VMEM] * len(operands),
        out_specs=[VMEM] * len(outs),
        compiler_params=PARAMS,
        cost_estimate=pl.CostEstimate(flops=1, bytes_accessed=1, transcendentals=0),
        name=name,
    )(*operands)


def gc_taper(r):
    near = 1.0 + r * r * (-5.0 / 3.0 + r * (0.625 + r * (0.5 - 0.25 * r)))
    s = jnp.maximum(r, 1.0)
    far = 4.0 - 5.0 * s + s * s * (5.0 / 3.0 + s * (0.625 + s * (s * (1.0 / 12.0) - 0.5))) - (2.0 / 3.0) / s
    return jnp.where(r <= 1.0, near, jnp.where(r <= 2.0, far, 0.0))


def prepare_kernel(x, coord, low, high):
    members, width = x.shape
    first = 4 * width * lax.axis_index("mesh")
    jitter = coord[...] - first - 4 * lax.broadcasted_iota(jnp.int32, (1, width), 1)
    pad = jnp.broadcast_to(jitter.astype(F32), (PAD, width)).astype(x.dtype)
    half = width // 2
    for part, span in ((low, slice(0, half)), (high, slice(half, width))):
        part[:members, :] = x[:, span]
        part[members:, :] = pad[:, span]


def own_kernel(x, coord, level, lt, row_coord, row_level, *outs, owned, split):
    members, width = x.shape
    groups = width // owned
    mem = lax.axis_index("mem")
    for part in range(groups):
        if split:
            start = pl.multiple_of(lax.rem(mem + 1 + part, groups) * owned, owned)
        else:
            start = part * owned
        lt[part * owned : (part + 1) * owned, :] = x[:, pl.ds(start, owned)].T
    tile = jnp.dot(lt[...], x[...], preferred_element_type=F32)
    store_rows(tile, outs, 0)
    rows = jnp.concatenate(
        [jnp.broadcast_to(coord[...], (CHUNK, width)), jnp.broadcast_to(level[...], (CHUNK, width))], axis=0
    )
    rows = rows.astype(F32)
    for part in range(groups):

        @pl.when(mem == part)
        def _():
            span = slice(part * owned, (part + 1) * owned)
            row_coord[...] = rows[:CHUNK, span].T
            row_level[...] = 0.05 * rows[CHUNK:, span].T


def store_rows(tile, outs, at):
    first = 0
    for out in outs:
        out[:, at : at + tile.shape[1]] = tile[first : first + out.shape[0]]
        first += out.shape[0]


def own_tile(x, coord, level, owned, rows):
    members, width = x.shape
    return call(
        functools.partial(own_kernel, owned=owned, split=len(rows) > 1),
        [jax.ShapeDtypeStruct((width, members), x.dtype)]
        + [jax.ShapeDtypeStruct((owned, CHUNK), F32)] * 2
        + [jax.ShapeDtypeStruct((r, width), F32) for r in rows],
        x,
        coord,
        level,
        name="own_tile",
        flops=2 * members * width * width,
    )


def narrowed(block):
    top = jnp.maximum(jnp.max(jnp.abs(block), axis=0, keepdims=True), 2.0**-126)
    power = jnp.ceil(8.0 * jnp.log2(top) + 0.01)
    steps = jnp.round(block * jnp.exp2(-0.125 * power) * STEPS)
    return steps.astype(jnp.int32), power.astype(jnp.int32)


def widened(steps, power):
    return (steps.astype(F32) * jnp.exp2(0.125 * power.astype(F32) - 16.0)) * (65536.0 / STEPS)


def pack(tile, packed):
    rows = tile.shape[0]
    for at in range(0, tile.shape[1] // 2, CHUNK):
        span = slice(at, at + CHUNK)
        high, high_power = narrowed(tile[:, 2 * at : 2 * at + CHUNK])
        low, low_power = narrowed(tile[:, 2 * at + CHUNK : 2 * at + 2 * CHUNK])
        packed[:rows, span] = (high << 16) | (low & 0xFFFF)
        packed[rows : rows + 4, span] = jnp.broadcast_to(high_power, (4, CHUNK))
        packed[rows + 4 :, span] = jnp.broadcast_to(low_power, (4, CHUNK))


def unpack(packed, block, rows):
    span = slice((block // 2) * CHUNK, (block // 2 + 1) * CHUNK)
    words = packed[:rows, span]
    if block % 2 == 0:
        return widened(words >> 16, packed[rows : rows + 1, span])
    return widened((words << 16) >> 16, packed[rows + 4 : rows + 5, span])


def panel_kernel(lt, *refs, picks, count, rows):
    panels, cols, outs = refs[:count], refs[count], refs[count + 1 :]
    members = lt.shape[1]

    def run(which):
        chosen = [panels[i] for i in which]
        at = 0
        for panel in chosen:
            wide = panel.shape[1]
            cols[:, at : at + wide] = panel[members:, :].astype(F32)[:8]
            at += wide
        block = jnp.concatenate([panel[:members, :] for panel in chosen], axis=1)
        tile = jnp.dot(lt[...], block, preferred_element_type=F32)
        if len(rows) > 1:
            pack(tile[: rows[0]], outs[0])
            outs[1][...] = tile[rows[0] :]
        else:
            outs[0][...] = tile

    if len(picks) == 1:
        run(picks[0])
    else:
        cross = lax.rem(lax.axis_index("mesh") // 2, 2)
        for value, which in enumerate(picks):
            pl.when(cross == value)(functools.partial(run, which))


def panel_tile(lt, panels, picks, rows):
    wide = sum(panels[i].shape[1] for i in picks[0])
    width, members = lt.shape
    return call(
        functools.partial(panel_kernel, picks=picks, count=len(panels), rows=rows),
        [jax.ShapeDtypeStruct((8, wide), F32)]
        + ([jax.ShapeDtypeStruct((rows[0] + 8, wide // 2), jnp.int32)] if len(rows) > 1 else [])
        + [jax.ShapeDtypeStruct((rows[-1], wide), F32)],
        lt,
        *panels,
        name="panel_tile",
        flops=2 * members * width * wide,
    )


def finish_kernel(row_coord, row_level, *refs, plan, period, width, members, first):
    operands = sum(1 + n for n, _ in plan)
    out, scratch, sems = refs[-3], refs[-2], refs[-1]
    me = lax.axis_index("mesh")
    count = lax.axis_size("mesh")
    odd = lax.rem(me, 2)
    coord, level = row_coord[...], row_level[...]
    steps = {"own": 0, "two": 2, "extra": 1 + 2 * odd, "other": 3 - 2 * odd}
    copies = []
    at, slot = 0, 0
    for n, spans in plan:
        cols, parts = refs[at], refs[at + 1 : at + 1 + n]
        at += 1 + n
        for offset, wide, kind, inside in spans:
            step = steps[kind]
            base = (4 * (lax.rem(me + step, count) * width + inside)).astype(F32)
            for piece in range(0, wide, CHUNK):
                span = slice(offset + piece, offset + piece + CHUNK)
                raw = parts[0][:, span]
                for part in parts[1:]:
                    if part.dtype == jnp.int32:
                        raw = raw + unpack(part, span.start // CHUNK, raw.shape[0])
                    else:
                        raw = raw + part[:, span]
                place = 4 * (piece + lax.broadcasted_iota(jnp.int32, (1, CHUNK), 1))
                column = cols[0:1, span] + (base + place.astype(F32))
                gap = jnp.abs(column - coord)
                dist = jnp.minimum(gap, period - gap)
                c = gc_taper(dist * (1.0 / (12 * width))) * (raw * (1.0 / (members - 1)))
                scratch[:, slot * CHUNK : (slot + 1) * CHUNK] = c - jnp.clip(c, -level, level)
                slot += 1
            begin = (slot * CHUNK) - wide
            target = pl.multiple_of(step * width + inside, CHUNK)
            copy = pltpu.make_async_copy(
                scratch.at[:, begin : begin + wide], out.at[:, pl.ds(target, wide)], sems.at[len(copies)]
            )
            copy.start()
            copies.append(copy)
    for copy in copies:
        copy.wait()


def finish(row_coord, row_level, groups, out, shape, period, width, members):
    operands = [row_coord, row_level]
    plan, wide, copies = [], 0, 0
    for cols, parts, spans in groups:
        operands += [cols, *parts]
        plan.append((len(parts), spans))
        wide += sum(s[1] for s in spans)
        copies += len(spans)
    specs = [VMEM] * len(operands)
    aliases = {}
    if out is not None:
        aliases = {len(operands): 0}
        operands.append(out)
        specs.append(pl.BlockSpec(memory_space=pl.ANY))
    owned = shape[0]
    return pl.pallas_call(
        functools.partial(
            finish_kernel, plan=plan, period=period, width=width, members=members, first=out is None
        ),
        out_shape=jax.ShapeDtypeStruct(shape, F32),
        in_specs=specs,
        out_specs=pl.BlockSpec(memory_space=pl.ANY),
        scratch_shapes=[pltpu.VMEM((owned, wide), F32), pltpu.SemaphoreType.DMA((copies,))],
        input_output_aliases=aliases,
        compiler_params=PARAMS,
        cost_estimate=pl.CostEstimate(flops=1, bytes_accessed=1, transcendentals=0),
        name="finish",
    )(*operands)


def per_device(perturbations, node_coord, threshold_level):
    members, width = perturbations.shape
    groups = lax.axis_size("mem")
    count = lax.axis_size("mesh")
    period = 4.0 * width * count
    owned = width // groups
    everyone = members * groups
    split = groups == 2
    rows = [owned] * groups if split else [width]
    shape = (owned, 4 * width)
    coord = node_coord.reshape(1, width)
    levels = threshold_level.reshape(1, width)

    def permute(array, pairs):
        return lax.ppermute(array, "mesh", pairs)

    everywhere = range(count)
    swap_x = [(p, p ^ 2) for p in everywhere]
    relay = [(p, (p - 4) % count) if p % 4 >= 2 else (p, p ^ 1) for p in everywhere]
    far_siblings = [(p, p ^ 1) for p in everywhere if p % 4 >= 2]
    back_two = [(p, (p - 2) % count) for p in everywhere]
    siblings = [(p, p ^ 1) for p in everywhere]
    extra_pairs = [(p, p - 1) if p % 2 else (p, (p - 3) % count) for p in everywhere]

    def reduced(parts):
        if split:
            return [parts[1], lax.ppermute(parts[0], "mem", [(0, 1), (1, 0)])]
        return [lax.psum_scatter(parts[0], "mem", scatter_dimension=0, tiled=True)]

    half = width // 2
    low, high = call(
        prepare_kernel,
        [jax.ShapeDtypeStruct((members + PAD, half), perturbations.dtype)] * 2,
        perturbations,
        coord,
        name="prepare",
    )
    lt, row_coord, row_level, *own = own_tile(after(perturbations, low), coord, levels, owned, rows)
    own_parts = reduced(own)
    own_cols = jnp.concatenate([low[members : members + 8], high[members : members + 8]], axis=1).astype(F32)

    first = permute(low, swap_x)
    extra = [permute(a, extra_pairs) for a in (low, high)]
    straight = permute(after(high, first), back_two)
    passed = permute(first, relay)

    def tile(panels, picks, *tokens):
        return panel_tile(after(lt, *tokens), panels, picks, rows)

    def finished(out, token, *groups):
        groups = [(after(groups[0][0], token), *groups[0][1:])] + list(groups[1:])
        return finish(row_coord, row_level, groups, out, shape, period, width, everyone)

    extra_cols, *extra_parts = tile(extra, [[0, 1]], own_parts[-1])
    extra_parts = reduced(extra_parts)
    other = permute(after(straight, extra_parts[-1]), siblings)
    far = permute(passed, far_siblings)
    two_cols, *two_parts = tile([first, passed, straight], [[0, 2], [1, 2]], extra_cols)
    two_parts = reduced(two_parts)
    out = finished(
        None,
        two_cols,
        (own_cols, own_parts, [(0, width, "own", 0)]),
        (extra_cols, extra_parts, [(0, width, "extra", 0)]),
    )
    other_cols, *other_parts = tile([passed, far, other], [[0, 2], [1, 2]], two_cols)
    other_parts[0] = after(other_parts[0], out, two_parts[-1])
    other_parts = reduced(other_parts)
    out = finished(out, other_cols, (two_cols, two_parts, [(0, width, "two", 0)]))
    return finished(out, other_cols, (other_cols, other_parts, [(0, width, "other", 0)]))


def solution(mesh):
    in_specs = (P("mem", "mesh"), P("mesh"), P("mesh"))
    out_specs = P(("mesh", "mem"), None)
    return jax.shard_map(
        per_device, mesh=mesh, in_specs=in_specs, out_specs=out_specs, check_vma=False
    )
```

```python
import functools

import jax
import jax.numpy as jnp
from jax import lax
from jax.experimental import pallas as pl
from jax.experimental.pallas import tpu as pltpu
from jax.sharding import PartitionSpec as P

PAD = 16
STEPS = 32766.0
CHUNK = 128
PARAMS = pltpu.CompilerParams(vmem_limit_bytes=32 * 1024 * 1024)
VMEM = pl.BlockSpec(memory_space=pltpu.VMEM)
F32 = jnp.float32


def after(value, *tokens):
    return lax.optimization_barrier((value, *tokens))[0]


def call(kernel, outs, *operands, name, flops=0):
    size = sum(o.size * o.dtype.itemsize for o in (*outs, *operands))
    return pl.pallas_call(
        kernel,
        out_shape=outs,
        in_specs=[VMEM] * len(operands),
        out_specs=[VMEM] * len(outs),
        compiler_params=PARAMS,
        cost_estimate=pl.CostEstimate(flops=1, bytes_accessed=1, transcendentals=0),
        name=name,
    )(*operands)


def gc_taper(r):
    near = 1.0 + r * r * (-5.0 / 3.0 + r * (0.625 + r * (0.5 - 0.25 * r)))
    s = jnp.maximum(r, 1.0)
    far = 4.0 - 5.0 * s + s * s * (5.0 / 3.0 + s * (0.625 + s * (s * (1.0 / 12.0) - 0.5))) - (2.0 / 3.0) / s
    return jnp.where(r <= 1.0, near, jnp.where(r <= 2.0, far, 0.0))


def prepare_kernel(x, coord, high):
    members, width = x.shape
    half = width // 2
    first = 4 * width * lax.axis_index("mesh")
    jitter = coord[...] - first - 4 * lax.broadcasted_iota(jnp.int32, (1, width), 1)
    jitter = jitter.astype(F32)
    high[:members, :] = x[:, half:]
    high[members:, :] = jnp.concatenate(
        [jnp.broadcast_to(jitter[:, :half], (PAD // 2, half)), jnp.broadcast_to(jitter[:, half:], (PAD // 2, half))],
        axis=0,
    ).astype(x.dtype)


def prepare(x, coord):
    members, width = x.shape
    half = jax.ShapeDtypeStruct((members + PAD, width // 2), x.dtype)
    return call(prepare_kernel, [half], x, coord, name="prepare")[0]


def own_kernel(low, high, coord, level, lt, row_coord, row_level, *outs, owned, split):
    width, members = lt.shape
    groups = width // owned
    half = width // 2
    mem = lax.axis_index("mem")
    for at, part in ((0, low), (half, high)):
        columns = part[:members, :].T
        if split:
            begin = lax.rem(mem + 1 + at // half, 2) * half
            lt[pl.ds(pl.multiple_of(begin, half), half), :] = columns
        else:
            lt[at : at + half, :] = columns
    for at, part in ((0, low), (half, high)):
        tile = jnp.dot(lt[...], part[:members, :], preferred_element_type=F32)
        store_rows(tile, outs, at)
    rows = jnp.concatenate(
        [jnp.broadcast_to(coord[...], (CHUNK, width)), jnp.broadcast_to(level[...], (CHUNK, width))], axis=0
    )
    rows = rows.astype(F32)
    for part in range(groups):

        @pl.when(mem == part)
        def _():
            span = slice(part * owned, (part + 1) * owned)
            row_coord[...] = rows[:CHUNK, span].T
            row_level[...] = 0.05 * rows[CHUNK:, span].T


def store_rows(tile, outs, at):
    first = 0
    for out in outs:
        out[:, at : at + tile.shape[1]] = tile[first : first + out.shape[0]]
        first += out.shape[0]


def own_tile(low, high, coord, level, owned, rows):
    members, width = low.shape[0], 2 * low.shape[1]
    return call(
        functools.partial(own_kernel, owned=owned, split=len(rows) > 1),
        [jax.ShapeDtypeStruct((width, members), low.dtype)]
        + [jax.ShapeDtypeStruct((owned, CHUNK), F32)] * 2
        + [jax.ShapeDtypeStruct((r, width), F32) for r in rows],
        low,
        high,
        coord,
        level,
        name="own_tile",
        flops=2 * members * width * width,
    )


def narrowed(block):
    top = jnp.maximum(jnp.max(jnp.abs(block), axis=0, keepdims=True), 2.0**-126)
    power = jnp.ceil(8.0 * jnp.log2(top) + 0.01)
    steps = jnp.round(block * jnp.exp2(-0.125 * power) * STEPS)
    return steps.astype(jnp.int32), power.astype(jnp.int32)


def widened(steps, power):
    return (steps.astype(F32) * jnp.exp2(0.125 * power.astype(F32) - 16.0)) * (65536.0 / STEPS)


def pack(tile, packed):
    rows = tile.shape[0]
    for at in range(0, tile.shape[1] // 2, CHUNK):
        span = slice(at, at + CHUNK)
        high, high_power = narrowed(tile[:, 2 * at : 2 * at + CHUNK])
        low, low_power = narrowed(tile[:, 2 * at + CHUNK : 2 * at + 2 * CHUNK])
        packed[:rows, span] = (high << 16) | (low & 0xFFFF)
        packed[rows : rows + 4, span] = jnp.broadcast_to(high_power, (4, CHUNK))
        packed[rows + 4 :, span] = jnp.broadcast_to(low_power, (4, CHUNK))


def unpack(packed, block, rows):
    span = slice((block // 2) * CHUNK, (block // 2 + 1) * CHUNK)
    words = packed[:rows, span]
    if block % 2 == 0:
        return widened(words >> 16, packed[rows : rows + 1, span])
    return widened((words << 16) >> 16, packed[rows + 4 : rows + 5, span])


def panel_kernel(lt, *refs, picks, count, rows, keep):
    panels, cols, outs = refs[:count], refs[count], refs[count + 1 :]
    members = lt.shape[1]

    def run(which):
        chosen = [panels[i] for i in which]
        half = cols.shape[1] // 2
        pad = [chosen[-1][members:, :].astype(F32)] * 2
        if len(chosen) == 1:
            pad = [pad[0][:, :half], pad[0][:, half:]]
        cols[:, :half] = pad[0][: PAD // 2]
        cols[:, half:] = pad[1][PAD // 2 :]
        if keep:
            for at, panel in zip((0, half), chosen):
                outs[-1][:members, at : at + half] = panel[:members, :]
                outs[-1][members:, at : at + half] = chosen[-1][members:, :]
        block = jnp.concatenate([panel[:members, :] for panel in chosen], axis=1)
        tile = jnp.dot(lt[...], block, preferred_element_type=F32)
        if len(rows) > 1:
            pack(tile[: rows[0]], outs[0])
            outs[1][...] = tile[rows[0] :]
        else:
            outs[0][...] = tile

    if len(picks) == 1:
        run(picks[0])
    else:
        cross = lax.rem(lax.axis_index("mesh") // 2, 2)
        for value, which in enumerate(picks):
            pl.when(cross == value)(functools.partial(run, which))


def panel_tile(lt, panels, picks, rows, keep=False):
    wide = sum(panels[i].shape[1] for i in picks[0])
    width, members = lt.shape
    return call(
        functools.partial(panel_kernel, picks=picks, count=len(panels), rows=rows, keep=keep),
        [jax.ShapeDtypeStruct((8, wide), F32)]
        + ([jax.ShapeDtypeStruct((rows[0] + 8, wide // 2), jnp.int32)] if len(rows) > 1 else [])
        + [jax.ShapeDtypeStruct((rows[-1], wide), F32)]
        + ([jax.ShapeDtypeStruct((members + PAD, wide), lt.dtype)] if keep else []),
        lt,
        *panels,
        name="panel_tile",
        flops=2 * members * width * wide,
    )


def finish_kernel(row_coord, row_level, *refs, plan, period, width, members, first):
    operands = sum(1 + n for n, _ in plan)
    out, scratch, sems = refs[-3], refs[-2], refs[-1]
    me = lax.axis_index("mesh")
    count = lax.axis_size("mesh")
    odd = lax.rem(me, 2)
    coord, level = row_coord[...], row_level[...]
    steps = {"own": 0, "two": 2, "extra": 1 + 2 * odd, "other": 3 - 2 * odd}
    copies = []
    at, slot = 0, 0
    for n, spans in plan:
        cols, parts = refs[at], refs[at + 1 : at + 1 + n]
        at += 1 + n
        for offset, wide, kind, inside in spans:
            step = steps[kind]
            base = (4 * (lax.rem(me + step, count) * width + inside)).astype(F32)
            for piece in range(0, wide, CHUNK):
                span = slice(offset + piece, offset + piece + CHUNK)
                raw = parts[0][:, span]
                for part in parts[1:]:
                    if part.dtype == jnp.int32:
                        raw = raw + unpack(part, span.start // CHUNK, raw.shape[0])
                    else:
                        raw = raw + part[:, span]
                place = 4 * (piece + lax.broadcasted_iota(jnp.int32, (1, CHUNK), 1))
                column = cols[0:1, span] + (base + place.astype(F32))
                gap = jnp.abs(column - coord)
                dist = jnp.minimum(gap, period - gap)
                c = gc_taper(dist * (1.0 / (12 * width))) * (raw * (1.0 / (members - 1)))
                scratch[:, slot * CHUNK : (slot + 1) * CHUNK] = c - jnp.clip(c, -level, level)
                slot += 1
            begin = (slot * CHUNK) - wide
            target = pl.multiple_of(step * width + inside, CHUNK)
            copy = pltpu.make_async_copy(
                scratch.at[:, begin : begin + wide], out.at[:, pl.ds(target, wide)], sems.at[len(copies)]
            )
            copy.start()
            copies.append(copy)
    for copy in copies:
        copy.wait()


def finish(row_coord, row_level, groups, out, shape, period, width, members):
    operands = [row_coord, row_level]
    plan, wide, copies = [], 0, 0
    for cols, parts, spans in groups:
        operands += [cols, *parts]
        plan.append((len(parts), spans))
        wide += sum(s[1] for s in spans)
        copies += len(spans)
    specs = [VMEM] * len(operands)
    aliases = {}
    if out is not None:
        aliases = {len(operands): 0}
        operands.append(out)
        specs.append(pl.BlockSpec(memory_space=pl.ANY))
    owned = shape[0]
    return pl.pallas_call(
        functools.partial(
            finish_kernel, plan=plan, period=period, width=width, members=members, first=out is None
        ),
        out_shape=jax.ShapeDtypeStruct(shape, F32),
        in_specs=specs,
        out_specs=pl.BlockSpec(memory_space=pl.ANY),
        scratch_shapes=[pltpu.VMEM((owned, wide), F32), pltpu.SemaphoreType.DMA((copies,))],
        input_output_aliases=aliases,
        compiler_params=PARAMS,
        cost_estimate=pl.CostEstimate(flops=1, bytes_accessed=1, transcendentals=0),
        name="finish",
    )(*operands)


def per_device(perturbations, node_coord, threshold_level):
    members, width = perturbations.shape
    groups = lax.axis_size("mem")
    count = lax.axis_size("mesh")
    period = 4.0 * width * count
    owned = width // groups
    everyone = members * groups
    split = groups == 2
    rows = [owned] * groups if split else [width]
    shape = (owned, 4 * width)
    coord = node_coord.reshape(1, width)
    levels = threshold_level.reshape(1, width)

    def permute(array, pairs):
        return lax.ppermute(array, "mesh", pairs)

    everywhere = range(count)
    swap_x = [(p, p ^ 2) for p in everywhere]
    relay = [(p, (p - 4) % count) for p in everywhere if p % 4 >= 2]
    back_two = [(p, (p - 2) % count) for p in everywhere]
    siblings = [(p, p ^ 1) for p in everywhere]
    extra_pairs = [(p, p - 1) if p % 2 else (p, (p - 3) % count) for p in everywhere]

    def reduced(parts):
        if split:
            return [parts[1], lax.ppermute(parts[0], "mem", [(0, 1), (1, 0)])]
        return [lax.psum_scatter(parts[0], "mem", scatter_dimension=0, tiled=True)]

    half = width // 2
    low = perturbations[:, :half]
    high = prepare(after(perturbations, low), coord)
    lt, row_coord, row_level, *own = own_tile(low, high, coord, levels, owned, rows)
    own_parts = reduced(own)
    own_cols = jnp.concatenate([high[members : members + PAD // 2], high[members + PAD // 2 :]], axis=1).astype(F32)

    first = permute(low, swap_x)
    extra = [permute(a, extra_pairs) for a in (low, high)]
    straight = permute(after(high, first), back_two)
    passed = permute(first, relay)

    def tile(panels, picks, *tokens, keep=False):
        return panel_tile(after(lt, *tokens), panels, picks, rows, keep)

    def finished(out, token, *groups):
        groups = [(after(groups[0][0], token), *groups[0][1:])] + list(groups[1:])
        return finish(row_coord, row_level, groups, out, shape, period, width, everyone)

    extra_cols, *extra_parts = tile(extra, [[0, 1]], own_parts[-1])
    extra_parts = reduced(extra_parts)
    out = finished(
        None,
        extra_cols,
        (own_cols, own_parts, [(0, width, "own", 0)]),
        (extra_cols, extra_parts, [(0, width, "extra", 0)]),
    )
    two_cols, *two_parts, two = tile([first, passed, straight], [[0, 2], [1, 2]], out, keep=True)
    two_parts = reduced(two_parts)
    other = permute(two, siblings)
    other_cols, *other_parts = tile([other], [[0]])
    other_parts = reduced(other_parts)
    out = finished(out, other_cols, (two_cols, two_parts, [(0, width, "two", 0)]))
    return finished(out, other_cols, (other_cols, other_parts, [(0, width, "other", 0)]))


def solution(mesh):
    in_specs = (P("mem", "mesh"), P("mesh"), P("mesh"))
    out_specs = P(("mesh", "mem"), None)
    return jax.shard_map(
        per_device, mesh=mesh, in_specs=in_specs, out_specs=out_specs, check_vma=False
    )
```

```python
import functools

import jax
import jax.numpy as jnp
from jax import lax
from jax.experimental import pallas as pl
from jax.experimental.pallas import tpu as pltpu
from jax.sharding import PartitionSpec as P

PAD = 16
STEPS = 32766.0
CHUNK = 128
PARAMS = pltpu.CompilerParams(vmem_limit_bytes=32 * 1024 * 1024)
VMEM = pl.BlockSpec(memory_space=pltpu.VMEM)
F32 = jnp.float32


def after(value, *tokens):
    return lax.optimization_barrier((value, *tokens))[0]


def call(kernel, outs, *operands, name, flops=0):
    size = sum(o.size * o.dtype.itemsize for o in (*outs, *operands))
    return pl.pallas_call(
        kernel,
        out_shape=outs,
        in_specs=[VMEM] * len(operands),
        out_specs=[VMEM] * len(outs),
        compiler_params=PARAMS,
        cost_estimate=pl.CostEstimate(flops=1, bytes_accessed=1, transcendentals=0),
        name=name,
    )(*operands)


def gc_taper(r):
    near = 1.0 + r * r * (-5.0 / 3.0 + r * (0.625 + r * (0.5 - 0.25 * r)))
    s = jnp.maximum(r, 1.0)
    far = 4.0 - 5.0 * s + s * s * (5.0 / 3.0 + s * (0.625 + s * (s * (1.0 / 12.0) - 0.5))) - (2.0 / 3.0) / s
    return jnp.where(r <= 1.0, near, jnp.where(r <= 2.0, far, 0.0))


def prepare_kernel(x, coord, high):
    members, width = x.shape
    half = width // 2
    first = 4 * width * lax.axis_index("mesh")
    jitter = coord[...] - first - 4 * lax.broadcasted_iota(jnp.int32, (1, width), 1)
    jitter = jitter.astype(F32)
    high[:members, :] = x[:, half:]
    high[members:, :] = jnp.concatenate(
        [jnp.broadcast_to(jitter[:, :half], (PAD // 2, half)), jnp.broadcast_to(jitter[:, half:], (PAD // 2, half))],
        axis=0,
    ).astype(x.dtype)


def prepare(x, coord):
    members, width = x.shape
    half = jax.ShapeDtypeStruct((members + PAD, width // 2), x.dtype)
    return call(prepare_kernel, [half], x, coord, name="prepare")[0]


def own_kernel(low, high, coord, level, lt, row_coord, row_level, *outs, owned, split):
    width, members = lt.shape
    groups = width // owned
    half = width // 2
    mem = lax.axis_index("mem")
    for at, part in ((0, low), (half, high)):
        columns = part[:members, :].T
        if split:
            begin = lax.rem(mem + 1 + at // half, 2) * half
            lt[pl.ds(pl.multiple_of(begin, half), half), :] = columns
        else:
            lt[at : at + half, :] = columns
    for at, part in ((0, low), (half, high)):
        tile = jnp.dot(lt[...], part[:members, :], preferred_element_type=F32)
        store_rows(tile, outs, at)
    rows = jnp.concatenate(
        [jnp.broadcast_to(coord[...], (CHUNK, width)), jnp.broadcast_to(level[...], (CHUNK, width))], axis=0
    )
    rows = rows.astype(F32)
    for part in range(groups):

        @pl.when(mem == part)
        def _():
            span = slice(part * owned, (part + 1) * owned)
            row_coord[...] = rows[:CHUNK, span].T
            row_level[...] = 0.05 * rows[CHUNK:, span].T


def store_rows(tile, outs, at):
    first = 0
    for out in outs:
        out[:, at : at + tile.shape[1]] = tile[first : first + out.shape[0]]
        first += out.shape[0]


def own_tile(low, high, coord, level, owned, rows):
    members, width = low.shape[0], 2 * low.shape[1]
    return call(
        functools.partial(own_kernel, owned=owned, split=len(rows) > 1),
        [jax.ShapeDtypeStruct((width, members), low.dtype)]
        + [jax.ShapeDtypeStruct((owned, CHUNK), F32)] * 2
        + [jax.ShapeDtypeStruct((r, width), F32) for r in rows],
        low,
        high,
        coord,
        level,
        name="own_tile",
        flops=2 * members * width * width,
    )


def narrowed(block):
    top = jnp.maximum(jnp.max(jnp.abs(block), axis=0, keepdims=True), 2.0**-126)
    power = jnp.ceil(8.0 * jnp.log2(top) + 0.01)
    steps = jnp.round(block * jnp.exp2(-0.125 * power) * STEPS)
    return steps.astype(jnp.int32), power.astype(jnp.int32)


def widened(steps, power):
    return (steps.astype(F32) * jnp.exp2(0.125 * power.astype(F32) - 16.0)) * (65536.0 / STEPS)


def pack(tile, packed):
    rows = tile.shape[0]
    for at in range(0, tile.shape[1] // 2, CHUNK):
        span = slice(at, at + CHUNK)
        high, high_power = narrowed(tile[:, 2 * at : 2 * at + CHUNK])
        low, low_power = narrowed(tile[:, 2 * at + CHUNK : 2 * at + 2 * CHUNK])
        packed[:rows, span] = (high << 16) | (low & 0xFFFF)
        packed[rows : rows + 4, span] = jnp.broadcast_to(high_power, (4, CHUNK))
        packed[rows + 4 :, span] = jnp.broadcast_to(low_power, (4, CHUNK))


def unpack(packed, block, rows):
    span = slice((block // 2) * CHUNK, (block // 2 + 1) * CHUNK)
    words = packed[:rows, span]
    if block % 2 == 0:
        return widened(words >> 16, packed[rows : rows + 1, span])
    return widened((words << 16) >> 16, packed[rows + 4 : rows + 5, span])


def panel_kernel(lt, *refs, picks, count, rows, keep):
    panels, cols, outs = refs[:count], refs[count], refs[count + 1 :]
    members = lt.shape[1]

    def run(which):
        chosen = [panels[i] for i in which]
        half = cols.shape[1] // 2
        pad = [chosen[-1][members:, :].astype(F32)] * 2
        if len(chosen) == 1:
            pad = [pad[0][:, :half], pad[0][:, half:]]
        cols[:, :half] = pad[0][: PAD // 2]
        cols[:, half:] = pad[1][PAD // 2 :]
        if keep:
            for at, panel in zip((0, half), chosen):
                outs[-1][:members, at : at + half] = panel[:members, :]
                outs[-1][members:, at : at + half] = chosen[-1][members:, :]
        block = jnp.concatenate([panel[:members, :] for panel in chosen], axis=1)
        tile = jnp.dot(lt[...], block, preferred_element_type=F32)
        if len(rows) > 1:
            pack(tile[: rows[0]], outs[0])
            outs[1][...] = tile[rows[0] :]
        else:
            outs[0][...] = tile

    if len(picks) == 1:
        run(picks[0])
    else:
        cross = lax.rem(lax.axis_index("mesh") // 2, 2)
        for value, which in enumerate(picks):
            pl.when(cross == value)(functools.partial(run, which))


def panel_tile(lt, panels, picks, rows, keep=False):
    wide = sum(panels[i].shape[1] for i in picks[0])
    width, members = lt.shape
    return call(
        functools.partial(panel_kernel, picks=picks, count=len(panels), rows=rows, keep=keep),
        [jax.ShapeDtypeStruct((8, wide), F32)]
        + ([jax.ShapeDtypeStruct((rows[0] + 8, wide // 2), jnp.int32)] if len(rows) > 1 else [])
        + [jax.ShapeDtypeStruct((rows[-1], wide), F32)]
        + ([jax.ShapeDtypeStruct((members + PAD, wide), lt.dtype)] if keep else []),
        lt,
        *panels,
        name="panel_tile",
        flops=2 * members * width * wide,
    )


def panel_steps():
    odd = lax.rem(lax.axis_index("mesh"), 2)
    return {"own": 0, "two": 2, "extra": 1 + 2 * odd, "other": 3 - 2 * odd}


def weight(offsets, row_coord, step, first, period, width, members):
    panel = lax.rem(lax.axis_index("mesh") + step, lax.axis_size("mesh"))
    base = (4 * (panel * width + first)).astype(F32)
    place = 4 * lax.broadcasted_iota(jnp.int32, (1, CHUNK), 1)
    gap = jnp.abs(offsets + (base + place.astype(F32)) - row_coord)
    dist = jnp.minimum(gap, period - gap)
    return gc_taper(dist * (1.0 / (12 * width))) * (1.0 / (members - 1))


def weigh_kernel(row_coord, cols, out, *, kind, period, width, members):
    step = panel_steps()[kind]
    for at in range(0, out.shape[1], CHUNK):
        span = slice(at, at + CHUNK)
        out[:, span] = weight(cols[0:1, span], row_coord[...], step, at, period, width, members)


def finish_kernel(row_coord, row_level, *refs, plan, period, width, members):
    out, scratch, sems = refs[-3], refs[-2], refs[-1]
    steps = panel_steps()
    coord, level = row_coord[...], row_level[...]
    copies = []
    at = 0
    for n, kind in plan:
        cols, parts = refs[at], refs[at + 1 : at + 1 + n]
        at += 1 + n
        step = steps[kind]
        for begin in range(0, width, CHUNK):
            span = slice(begin, begin + CHUNK)
            slot = len(copies)
            raw = parts[0][:, span]
            for part in parts[1:]:
                if part.dtype == jnp.int32:
                    raw = raw + unpack(part, begin // CHUNK, raw.shape[0])
                else:
                    raw = raw + part[:, span]
            if cols.shape[0] == out.shape[0]:
                scale = cols[:, span]
            else:
                scale = weight(cols[0:1, span], coord, step, begin, period, width, members)
            c = scale * raw
            scratch[slot] = c - jnp.clip(c, -level, level)
            target = pl.multiple_of(step * width + begin, CHUNK)
            copy = pltpu.make_async_copy(scratch.at[slot], out.at[:, pl.ds(target, CHUNK)], sems.at[slot])
            copy.start()
            copies.append(copy)
    for copy in copies:
        copy.wait()


def finish(row_coord, row_level, groups, out, shape, period, width, members):
    operands = [row_coord, row_level]
    plan = []
    for cols, parts, kind in groups:
        operands += [cols, *parts]
        plan.append((len(parts), kind))
    copies = len(plan) * (width // CHUNK)
    specs = [VMEM] * len(operands)
    aliases = {}
    if out is not None:
        aliases = {len(operands): 0}
        operands.append(out)
        specs.append(pl.BlockSpec(memory_space=pl.ANY))
    return pl.pallas_call(
        functools.partial(finish_kernel, plan=plan, period=period, width=width, members=members),
        out_shape=jax.ShapeDtypeStruct(shape, F32),
        in_specs=specs,
        out_specs=pl.BlockSpec(memory_space=pl.ANY),
        scratch_shapes=[pltpu.VMEM((copies, shape[0], CHUNK), F32), pltpu.SemaphoreType.DMA((copies,))],
        input_output_aliases=aliases,
        compiler_params=PARAMS,
        cost_estimate=pl.CostEstimate(flops=1, bytes_accessed=1, transcendentals=0),
        name="finish",
    )(*operands)


def per_device(perturbations, node_coord, threshold_level):
    members, width = perturbations.shape
    groups = lax.axis_size("mem")
    count = lax.axis_size("mesh")
    period = 4.0 * width * count
    owned = width // groups
    everyone = members * groups
    split = groups == 2
    rows = [owned] * groups if split else [width]
    shape = (owned, 4 * width)
    coord = node_coord.reshape(1, width)
    levels = threshold_level.reshape(1, width)

    def permute(array, pairs):
        return lax.ppermute(array, "mesh", pairs)

    everywhere = range(count)
    swap_x = [(p, p ^ 2) for p in everywhere]
    relay = [(p, (p - 4) % count) for p in everywhere if p % 4 >= 2]
    back_two = [(p, (p - 2) % count) for p in everywhere]
    siblings = [(p, p ^ 1) for p in everywhere]
    extra_pairs = [(p, p - 1) if p % 2 else (p, (p - 3) % count) for p in everywhere]

    def reduced(parts):
        if split:
            return [parts[1], lax.ppermute(parts[0], "mem", [(0, 1), (1, 0)])]
        return [lax.psum_scatter(parts[0], "mem", scatter_dimension=0, tiled=True)]

    half = width // 2
    low = perturbations[:, :half]
    high = prepare(after(perturbations, low), coord)
    lt, row_coord, row_level, *own = own_tile(low, high, coord, levels, owned, rows)
    own_parts = reduced(own)
    own_cols = jnp.concatenate([high[members : members + PAD // 2], high[members + PAD // 2 :]], axis=1).astype(F32)

    first = permute(low, swap_x)
    extra = [permute(a, extra_pairs) for a in (low, high)]
    straight = permute(after(high, first), back_two)
    passed = permute(first, relay)

    def tile(panels, picks, *tokens, keep=False):
        return panel_tile(after(lt, *tokens), panels, picks, rows, keep)

    def finished(out, token, *groups):
        groups = [(after(groups[0][0], token), *groups[0][1:])] + list(groups[1:])
        return finish(row_coord, row_level, groups, out, shape, period, width, everyone)

    extra_cols, *extra_parts = tile(extra, [[0, 1]], own_parts[-1])
    extra_parts = reduced(extra_parts)
    out = finished(None, extra_cols, (own_cols, own_parts, "own"), (extra_cols, extra_parts, "extra"))
    two_cols, *two_parts, two = tile([first, passed, straight], [[0, 2], [1, 2]], out, keep=True)
    two_parts = reduced(two_parts)
    other = permute(two, siblings)
    other_cols, *other_parts = tile([other], [[0]])
    other_parts = reduced(other_parts)
    weights = call(
        functools.partial(weigh_kernel, kind="other", period=period, width=width, members=everyone),
        [jax.ShapeDtypeStruct((owned, width), F32)],
        row_coord,
        other_cols,
        name="weigh",
    )[0]
    out = finished(out, weights, (two_cols, two_parts, "two"))
    return finished(out, other_cols, (weights, other_parts, "other"))


def solution(mesh):
    in_specs = (P("mem", "mesh"), P("mesh"), P("mesh"))
    out_specs = P(("mesh", "mem"), None)
    return jax.shard_map(
        per_device, mesh=mesh, in_specs=in_specs, out_specs=out_specs, check_vma=False
    )
```

```python
import functools

import jax
import jax.numpy as jnp
from jax import lax
from jax.experimental import pallas as pl
from jax.experimental.pallas import tpu as pltpu
from jax.sharding import PartitionSpec as P

PAD = 16
STEPS = 32766.0
CHUNK = 128
PARAMS = pltpu.CompilerParams(vmem_limit_bytes=32 * 1024 * 1024)
VMEM = pl.BlockSpec(memory_space=pltpu.VMEM)
F32 = jnp.float32


def after(value, *tokens):
    return lax.optimization_barrier((value, *tokens))[0]


def call(kernel, outs, *operands, name, flops=0):
    size = sum(o.size * o.dtype.itemsize for o in (*outs, *operands))
    return pl.pallas_call(
        kernel,
        out_shape=outs,
        in_specs=[VMEM] * len(operands),
        out_specs=[VMEM] * len(outs),
        compiler_params=PARAMS,
        cost_estimate=pl.CostEstimate(flops=1, bytes_accessed=1, transcendentals=0),
        name=name,
    )(*operands)


def gc_taper(r):
    near = 1.0 + r * r * (-5.0 / 3.0 + r * (0.625 + r * (0.5 - 0.25 * r)))
    s = jnp.maximum(r, 1.0)
    far = 4.0 - 5.0 * s + s * s * (5.0 / 3.0 + s * (0.625 + s * (s * (1.0 / 12.0) - 0.5))) - (2.0 / 3.0) / s
    return jnp.where(r <= 1.0, near, jnp.where(r <= 2.0, far, 0.0))


def prepare_kernel(x, coord, high, *parts):
    members, width = x.shape
    half = width // 2
    first = 4 * width * lax.axis_index("mesh")
    jitter = coord[...] - first - 4 * lax.broadcasted_iota(jnp.int32, (1, width), 1)
    jitter = jitter.astype(F32)
    high[:members, :] = x[:, half:]
    high[members:, :] = jnp.concatenate(
        [jnp.broadcast_to(jitter[:, :half], (PAD // 2, half)), jnp.broadcast_to(jitter[:, half:], (PAD // 2, half))],
        axis=0,
    ).astype(x.dtype)
    cut_kernel(high, *parts)


def cut_kernel(whole, *parts):
    wide = parts[0].shape[1]
    for i, part in enumerate(parts):
        part[...] = whole[:, i * wide : (i + 1) * wide]


def cut(panel):
    half = jax.ShapeDtypeStruct((panel.shape[0], panel.shape[1] // 2), panel.dtype)
    return call(cut_kernel, [half] * 2, panel, name="cut")


def prepare(x, coord):
    members, width = x.shape
    outs = [jax.ShapeDtypeStruct((members + PAD, w), x.dtype) for w in (width // 2, width // 4, width // 4)]
    return call(prepare_kernel, outs, x, coord, name="prepare")


def own_kernel(low, high, coord, level, lt, row_coord, row_level, *outs, owned, split):
    width, members = lt.shape
    groups = width // owned
    half = width // 2
    mem = lax.axis_index("mem")
    for at, part in ((0, low), (half, high)):
        columns = part[:members, :].T
        if split:
            begin = lax.rem(mem + 1 + at // half, 2) * half
            lt[pl.ds(pl.multiple_of(begin, half), half), :] = columns
        else:
            lt[at : at + half, :] = columns
    for at, part in ((0, low), (half, high)):
        tile = jnp.dot(lt[...], part[:members, :], preferred_element_type=F32)
        store_rows(tile, outs, at)
    rows = jnp.concatenate(
        [jnp.broadcast_to(coord[...], (CHUNK, width)), jnp.broadcast_to(level[...], (CHUNK, width))], axis=0
    )
    rows = rows.astype(F32)
    for part in range(groups):

        @pl.when(mem == part)
        def _():
            span = slice(part * owned, (part + 1) * owned)
            row_coord[...] = rows[:CHUNK, span].T
            row_level[...] = 0.05 * rows[CHUNK:, span].T


def store_rows(tile, outs, at):
    first = 0
    for out in outs:
        out[:, at : at + tile.shape[1]] = tile[first : first + out.shape[0]]
        first += out.shape[0]


def own_tile(low, high, coord, level, owned, rows):
    members, width = low.shape[0], 2 * low.shape[1]
    return call(
        functools.partial(own_kernel, owned=owned, split=len(rows) > 1),
        [jax.ShapeDtypeStruct((width, members), low.dtype)]
        + [jax.ShapeDtypeStruct((owned, CHUNK), F32)] * 2
        + [jax.ShapeDtypeStruct((r, width), F32) for r in rows],
        low,
        high,
        coord,
        level,
        name="own_tile",
        flops=2 * members * width * width,
    )


def narrowed(block):
    top = jnp.maximum(jnp.max(jnp.abs(block), axis=0, keepdims=True), 2.0**-126)
    power = jnp.ceil(8.0 * jnp.log2(top) + 0.01)
    steps = jnp.round(block * jnp.exp2(-0.125 * power) * STEPS)
    return steps.astype(jnp.int32), power.astype(jnp.int32)


def widened(steps, power):
    return (steps.astype(F32) * jnp.exp2(0.125 * power.astype(F32) - 16.0)) * (65536.0 / STEPS)


def pack(tile, packed):
    rows = tile.shape[0]
    for at in range(0, tile.shape[1] // 2, CHUNK):
        span = slice(at, at + CHUNK)
        high, high_power = narrowed(tile[:, 2 * at : 2 * at + CHUNK])
        low, low_power = narrowed(tile[:, 2 * at + CHUNK : 2 * at + 2 * CHUNK])
        packed[:rows, span] = (high << 16) | (low & 0xFFFF)
        packed[rows : rows + 4, span] = jnp.broadcast_to(high_power, (4, CHUNK))
        packed[rows + 4 :, span] = jnp.broadcast_to(low_power, (4, CHUNK))


def unpack(packed, block, rows):
    span = slice((block // 2) * CHUNK, (block // 2 + 1) * CHUNK)
    words = packed[:rows, span]
    if block % 2 == 0:
        return widened(words >> 16, packed[rows : rows + 1, span])
    return widened((words << 16) >> 16, packed[rows + 4 : rows + 5, span])


def panel_kernel(lt, *refs, picks, count, rows, pieces):
    panels, cols, outs = refs[:count], refs[count], refs[count + 1 :]
    members = lt.shape[1]

    def run(which):
        chosen = [panels[i] for i in which]
        half = cols.shape[1] // 2
        pad = [chosen[-1][members:, :].astype(F32)] * 2
        if len(chosen) == 1:
            pad = [pad[0][:, :half], pad[0][:, half:]]
        cols[:, :half] = pad[0][: PAD // 2]
        cols[:, half:] = pad[1][PAD // 2 :]
        block = jnp.concatenate([panel[:members, :] for panel in chosen], axis=1)
        tile = jnp.dot(lt[...], block, preferred_element_type=F32)
        if len(rows) > 1:
            wide = tile.shape[1] // pieces
            for i in range(pieces):
                pack(tile[: rows[0], i * wide : (i + 1) * wide], outs[i])
            outs[pieces][...] = tile[rows[0] :]
        else:
            outs[0][...] = tile

    if len(picks) == 1:
        run(picks[0])
    else:
        cross = lax.rem(lax.axis_index("mesh") // 2, 2)
        for value, which in enumerate(picks):
            pl.when(cross == value)(functools.partial(run, which))


def panel_tile(lt, panels, picks, rows, pieces=1):
    wide = sum(panels[i].shape[1] for i in picks[0])
    width, members = lt.shape
    outs = [jax.ShapeDtypeStruct((8, wide), F32)]
    if len(rows) > 1:
        outs += [jax.ShapeDtypeStruct((rows[0] + 8, wide // 2 // pieces), jnp.int32)] * pieces
    outs.append(jax.ShapeDtypeStruct((rows[-1], wide), F32))
    return call(
        functools.partial(panel_kernel, picks=picks, count=len(panels), rows=rows, pieces=pieces),
        outs,
        lt,
        *panels,
        name="panel_tile",
    )


def last_kernel(lt, near0, near1, far0, far1, straight0, straight1, cols, *refs, rows):
    outs, whole = refs[:-1], refs[-1]
    members = lt.shape[1]
    wide = near0.shape[1]

    def run(low0, low1):
        pad0, pad1 = straight0[members:, :], straight1[members:, :]
        for i, (panel, pad) in enumerate(((low0, pad0), (low1, pad1), (straight0, pad0), (straight1, pad1))):
            span = slice(i * wide, (i + 1) * wide)
            whole[:members, span] = panel[:members, :]
            whole[members:, span] = pad
        pad1 = pad1.astype(F32)
        cols[:, :wide] = pad1[: PAD // 2]
        cols[:, wide:] = pad1[PAD // 2 :]
        block = jnp.concatenate([low1[...], straight1[:members, :]], axis=1)
        tile = jnp.dot(lt[...], block, preferred_element_type=F32)
        if len(rows) > 1:
            pack(tile[: rows[0]], outs[0])
            outs[1][...] = tile[rows[0] :]
        else:
            outs[0][...] = tile

    cross = lax.rem(lax.axis_index("mesh") // 2, 2)
    pl.when(cross == 0)(lambda: run(near0, near1))
    pl.when(cross == 1)(lambda: run(far0, far1))


def last_tile(lt, panels, rows):
    width, members = lt.shape
    wide = width // 2
    return call(
        functools.partial(last_kernel, rows=rows),
        [jax.ShapeDtypeStruct((8, wide), F32)]
        + ([jax.ShapeDtypeStruct((rows[0] + 8, wide // 2), jnp.int32)] if len(rows) > 1 else [])
        + [jax.ShapeDtypeStruct((rows[-1], wide), F32), jax.ShapeDtypeStruct((members + PAD, width), lt.dtype)],
        lt,
        *panels,
        name="last_tile",
    )


def panel_steps():
    odd = lax.rem(lax.axis_index("mesh"), 2)
    return {"own": 0, "two": 2, "extra": 1 + 2 * odd, "other": 3 - 2 * odd}


def weight(offsets, row_coord, step, first, period, width, members):
    panel = lax.rem(lax.axis_index("mesh") + step, lax.axis_size("mesh"))
    base = (4 * (panel * width + first)).astype(F32)
    place = 4 * lax.broadcasted_iota(jnp.int32, (1, CHUNK), 1)
    gap = jnp.abs(offsets + (base + place.astype(F32)) - row_coord)
    dist = jnp.minimum(gap, period - gap)
    return gc_taper(dist * (1.0 / (12 * width))) * (1.0 / (members - 1))


def weigh_kernel(row_coord, cols, out, *, kind, period, width, members):
    step = panel_steps()[kind]
    for at in range(0, out.shape[1], CHUNK):
        span = slice(at, at + CHUNK)
        out[:, span] = weight(cols[0:1, span], row_coord[...], step, at, period, width, members)


def finish_kernel(row_coord, row_level, *refs, plan, period, width, members):
    out, scratch, sems = refs[-3], refs[-2], refs[-1]
    steps = panel_steps()
    coord, level = row_coord[...], row_level[...]
    copies = []
    at = 0
    for n, kind, starts in plan:
        cols, parts = refs[at], refs[at + 1 : at + 1 + n]
        at += 1 + n
        step = steps[kind]
        for block, begin in enumerate(starts):
            span = slice(block * CHUNK, (block + 1) * CHUNK)
            slot = len(copies)
            raw = parts[0][:, span]
            if len(parts) > 1:
                share = len(starts) // (len(parts) - 1)
                part = parts[1 + block // share]
                if part.dtype == jnp.int32:
                    raw = raw + unpack(part, block % share, raw.shape[0])
                else:
                    raw = raw + part[:, span]
            if cols.shape[0] == out.shape[0]:
                scale = cols[:, span]
            else:
                scale = weight(cols[0:1, span], coord, step, begin, period, width, members)
            c = scale * raw
            scratch[slot] = c - jnp.clip(c, -level, level)
            target = pl.multiple_of(step * width + begin, CHUNK)
            copy = pltpu.make_async_copy(scratch.at[slot], out.at[:, pl.ds(target, CHUNK)], sems.at[slot])
            copy.start()
            copies.append(copy)
    for copy in copies:
        copy.wait()


def finish(row_coord, row_level, groups, out, shape, period, width, members):
    operands = [row_coord, row_level]
    plan = []
    for cols, parts, kind, starts in groups:
        operands += [cols, *parts]
        plan.append((len(parts), kind, starts))
    copies = sum(len(starts) for _, _, starts in plan)
    specs = [VMEM] * len(operands)
    aliases = {}
    if out is not None:
        aliases = {len(operands): 0}
        operands.append(out)
        specs.append(pl.BlockSpec(memory_space=pl.ANY))
    return pl.pallas_call(
        functools.partial(finish_kernel, plan=plan, period=period, width=width, members=members),
        out_shape=jax.ShapeDtypeStruct(shape, F32),
        in_specs=specs,
        out_specs=pl.BlockSpec(memory_space=pl.ANY),
        scratch_shapes=[pltpu.VMEM((copies, shape[0], CHUNK), F32), pltpu.SemaphoreType.DMA((copies,))],
        input_output_aliases=aliases,
        compiler_params=PARAMS,
        cost_estimate=pl.CostEstimate(flops=1, bytes_accessed=1, transcendentals=0),
        name="finish",
    )(*operands)


def per_device(perturbations, node_coord, threshold_level):
    members, width = perturbations.shape
    groups = lax.axis_size("mem")
    count = lax.axis_size("mesh")
    period = 4.0 * width * count
    owned = width // groups
    everyone = members * groups
    split = groups == 2
    rows = [owned] * groups if split else [width]
    shape = (owned, 4 * width)
    coord = node_coord.reshape(1, width)
    levels = threshold_level.reshape(1, width)

    def permute(array, pairs):
        return lax.ppermute(array, "mesh", pairs)

    everywhere = range(count)
    swap_x = [(p, p ^ 2) for p in everywhere]
    relay = [(p, (p - 4) % count) for p in everywhere if p % 4 >= 2]
    back_two = [(p, (p - 2) % count) for p in everywhere]
    siblings = [(p, p ^ 1) for p in everywhere]
    extra_pairs = [(p, p - 1) if p % 2 else (p, (p - 3) % count) for p in everywhere]

    def reduced(parts):
        if split:
            return [parts[-1]] + [lax.ppermute(a, "mem", [(0, 1), (1, 0)]) for a in parts[:-1]]
        return [lax.psum_scatter(parts[0], "mem", scatter_dimension=0, tiled=True)]

    half = width // 2
    low = perturbations[:, :half]
    high, *highs = prepare(after(perturbations, low), coord)
    lt, row_coord, row_level, *own = own_tile(low, high, coord, levels, owned, rows)
    own_parts = reduced(own)
    own_cols = jnp.concatenate([high[members : members + PAD // 2], high[members + PAD // 2 :]], axis=1).astype(F32)

    first = permute(low, swap_x)
    extra = [permute(a, extra_pairs) for a in (low, high)]
    straight = [permute(after(a, first), back_two) for a in highs]
    near = cut(first)
    passed = [permute(a, relay) for a in near]

    def tile(panels, picks, *tokens, pieces=1):
        return panel_tile(after(lt, *tokens), panels, picks, rows, pieces)

    def finished(out, token, *groups):
        groups = [(after(groups[0][0], token), *groups[0][1:])] + list(groups[1:])
        return finish(row_coord, row_level, groups, out, shape, period, width, everyone)

    extra_cols, *extra_parts = tile(extra, [[0, 1]], own_parts[-1])
    extra_parts = reduced(extra_parts)
    early_cols, *early_parts = tile([near[0], passed[0], straight[0]], [[0, 2], [1, 2]], extra_cols)
    early_parts = reduced(early_parts)
    whole = [i * CHUNK for i in range(width // CHUNK)]
    out = finished(None, early_cols, (own_cols, own_parts, "own", whole), (extra_cols, extra_parts, "extra", whole))
    late_cols, *late_parts, two = last_tile(after(lt, out, early_parts[-1]), [*near, *passed, *straight], rows)
    late_parts = reduced(late_parts)
    other = permute(two, siblings)
    other_cols, *other_parts = tile([other], [[0]], pieces=2)
    other_parts = reduced(other_parts)
    weights = call(
        functools.partial(weigh_kernel, kind="other", period=period, width=width, members=everyone),
        [jax.ShapeDtypeStruct((owned, width), F32)],
        row_coord,
        other_cols,
        name="weigh",
    )[0]
    out = finished(
        out,
        weights,
        (early_cols, early_parts, "two", [0, half]),
        (late_cols, late_parts, "two", [CHUNK, half + CHUNK]),
    )
    return finished(out, other_cols, (weights, other_parts, "other", whole))


def solution(mesh):
    in_specs = (P("mem", "mesh"), P("mesh"), P("mesh"))
    out_specs = P(("mesh", "mem"), None)
    return jax.shard_map(
        per_device, mesh=mesh, in_specs=in_specs, out_specs=out_specs, check_vma=False
    )
```

```python
import functools

import jax
import jax.numpy as jnp
from jax import lax
from jax.experimental import pallas as pl
from jax.experimental.pallas import tpu as pltpu
from jax.sharding import PartitionSpec as P

PAD = 16
STEPS = 32766.0
CHUNK = 128
PARAMS = pltpu.CompilerParams(vmem_limit_bytes=32 * 1024 * 1024)
VMEM = pl.BlockSpec(memory_space=pltpu.VMEM)
F32 = jnp.float32


def after(value, *tokens):
    return lax.optimization_barrier((value, *tokens))[0]


def call(kernel, outs, *operands, name, flops=0):
    size = sum(o.size * o.dtype.itemsize for o in (*outs, *operands))
    return pl.pallas_call(
        kernel,
        out_shape=outs,
        in_specs=[VMEM] * len(operands),
        out_specs=[VMEM] * len(outs),
        compiler_params=PARAMS,
        cost_estimate=pl.CostEstimate(flops=1, bytes_accessed=1, transcendentals=0),
        name=name,
    )(*operands)


def gc_taper(r):
    near = 1.0 + r * r * (-5.0 / 3.0 + r * (0.625 + r * (0.5 - 0.25 * r)))
    s = jnp.maximum(r, 1.0)
    far = 4.0 - 5.0 * s + s * s * (5.0 / 3.0 + s * (0.625 + s * (s * (1.0 / 12.0) - 0.5))) - (2.0 / 3.0) / s
    return jnp.where(r <= 1.0, near, jnp.where(r <= 2.0, far, 0.0))


def prepare_kernel(x, coord, high, *parts):
    members, width = x.shape
    half = width // 2
    first = 4 * width * lax.axis_index("mesh")
    jitter = coord[...] - first - 4 * lax.broadcasted_iota(jnp.int32, (1, width), 1)
    jitter = jitter.astype(F32)
    high[:members, :] = x[:, half:]
    high[members:, :] = jnp.concatenate(
        [jnp.broadcast_to(jitter[:, :half], (PAD // 2, half)), jnp.broadcast_to(jitter[:, half:], (PAD // 2, half))],
        axis=0,
    ).astype(x.dtype)
    cut_kernel(high, *parts)


def cut_kernel(whole, *parts):
    wide = parts[0].shape[1]
    for i, part in enumerate(parts):
        part[...] = whole[:, i * wide : (i + 1) * wide]


def cut(panel):
    half = jax.ShapeDtypeStruct((panel.shape[0], panel.shape[1] // 2), panel.dtype)
    return call(cut_kernel, [half] * 2, panel, name="cut")


def prepare(x, coord):
    members, width = x.shape
    outs = [jax.ShapeDtypeStruct((members + PAD, w), x.dtype) for w in (width // 2, width // 4, width // 4)]
    return call(prepare_kernel, outs, x, coord, name="prepare")


def own_kernel(low, high, coord, level, lt, row_coord, row_level, *outs, owned, split):
    width, members = lt.shape
    groups = width // owned
    half = width // 2
    mem = lax.axis_index("mem")
    for at, part in ((0, low), (half, high)):
        columns = part[:members, :].T
        if split:
            begin = lax.rem(mem + 1 + at // half, 2) * half
            lt[pl.ds(pl.multiple_of(begin, half), half), :] = columns
        else:
            lt[at : at + half, :] = columns
    for at, part in ((0, low), (half, high)):
        tile = jnp.dot(lt[...], part[:members, :], preferred_element_type=F32)
        store_rows(tile, outs, at)
    rows = jnp.concatenate(
        [jnp.broadcast_to(coord[...], (CHUNK, width)), jnp.broadcast_to(level[...], (CHUNK, width))], axis=0
    )
    rows = rows.astype(F32)
    for part in range(groups):

        @pl.when(mem == part)
        def _():
            span = slice(part * owned, (part + 1) * owned)
            row_coord[...] = rows[:CHUNK, span].T
            row_level[...] = 0.05 * rows[CHUNK:, span].T


def store_rows(tile, outs, at):
    first = 0
    for out in outs:
        out[:, at : at + tile.shape[1]] = tile[first : first + out.shape[0]]
        first += out.shape[0]


def own_tile(low, high, coord, level, owned, rows):
    members, width = low.shape[0], 2 * low.shape[1]
    return call(
        functools.partial(own_kernel, owned=owned, split=len(rows) > 1),
        [jax.ShapeDtypeStruct((width, members), low.dtype)]
        + [jax.ShapeDtypeStruct((owned, CHUNK), F32)] * 2
        + [jax.ShapeDtypeStruct((r, width), F32) for r in rows],
        low,
        high,
        coord,
        level,
        name="own_tile",
        flops=2 * members * width * width,
    )


def narrowed(block):
    top = jnp.maximum(jnp.max(jnp.abs(block), axis=0, keepdims=True), 2.0**-126)
    power = jnp.ceil(8.0 * jnp.log2(top) + 0.01)
    steps = jnp.round(block * jnp.exp2(-0.125 * power) * STEPS)
    return steps.astype(jnp.int32), power.astype(jnp.int32)


def widened(steps, power):
    return (steps.astype(F32) * jnp.exp2(0.125 * power.astype(F32) - 16.0)) * (65536.0 / STEPS)


def pack(tile, packed):
    rows = tile.shape[0]
    for at in range(0, tile.shape[1] // 2, CHUNK):
        span = slice(at, at + CHUNK)
        high, high_power = narrowed(tile[:, 2 * at : 2 * at + CHUNK])
        low, low_power = narrowed(tile[:, 2 * at + CHUNK : 2 * at + 2 * CHUNK])
        packed[:rows, span] = (high << 16) | (low & 0xFFFF)
        packed[rows : rows + 4, span] = jnp.broadcast_to(high_power, (4, CHUNK))
        packed[rows + 4 :, span] = jnp.broadcast_to(low_power, (4, CHUNK))


def unpack(packed, block, rows):
    span = slice((block // 2) * CHUNK, (block // 2 + 1) * CHUNK)
    words = packed[:rows, span]
    if block % 2 == 0:
        return widened(words >> 16, packed[rows : rows + 1, span])
    return widened((words << 16) >> 16, packed[rows + 4 : rows + 5, span])


def panel_kernel(lt, *refs, picks, count, rows, keep):
    panels, cols, outs = refs[:count], refs[count], refs[count + 1 :]
    members = lt.shape[1]

    def run(which):
        chosen = [panels[i] for i in which]
        half = cols.shape[1] // 2
        pad = [chosen[-1][members:, :].astype(F32)] * 2
        if len(chosen) == 1:
            pad = [pad[0][:, :half], pad[0][:, half:]]
        cols[:, :half] = pad[0][: PAD // 2]
        cols[:, half:] = pad[1][PAD // 2 :]
        if keep:
            for at, panel in zip((0, half), chosen):
                outs[-1][:members, at : at + half] = panel[:members, :]
                outs[-1][members:, at : at + half] = chosen[-1][members:, :]
        block = jnp.concatenate([panel[:members, :] for panel in chosen], axis=1)
        tile = jnp.dot(lt[...], block, preferred_element_type=F32)
        if len(rows) > 1:
            pack(tile[: rows[0]], outs[0])
            outs[1][...] = tile[rows[0] :]
        else:
            outs[0][...] = tile

    if len(picks) == 1:
        run(picks[0])
    else:
        cross = lax.rem(lax.axis_index("mesh") // 2, 2)
        for value, which in enumerate(picks):
            pl.when(cross == value)(functools.partial(run, which))


def panel_tile(lt, panels, picks, rows, keep=False):
    wide = sum(panels[i].shape[1] for i in picks[0])
    width, members = lt.shape
    return call(
        functools.partial(panel_kernel, picks=picks, count=len(panels), rows=rows, keep=keep),
        [jax.ShapeDtypeStruct((8, wide), F32)]
        + ([jax.ShapeDtypeStruct((rows[0] + 8, wide // 2), jnp.int32)] if len(rows) > 1 else [])
        + [jax.ShapeDtypeStruct((rows[-1], wide), F32)]
        + ([jax.ShapeDtypeStruct((members + PAD, wide), lt.dtype)] if keep else []),
        lt,
        *panels,
        name="panel_tile",
    )


def panel_steps():
    odd = lax.rem(lax.axis_index("mesh"), 2)
    return {"own": 0, "two": 2, "extra": 1 + 2 * odd, "other": 3 - 2 * odd}


def weight(offsets, row_coord, step, first, period, width, members):
    panel = lax.rem(lax.axis_index("mesh") + step, lax.axis_size("mesh"))
    base = (4 * (panel * width + first)).astype(F32)
    place = 4 * lax.broadcasted_iota(jnp.int32, (1, CHUNK), 1)
    gap = jnp.abs(offsets + (base + place.astype(F32)) - row_coord)
    dist = jnp.minimum(gap, period - gap)
    return gc_taper(dist * (1.0 / (12 * width))) * (1.0 / (members - 1))


def weigh_kernel(row_coord, cols, out, *, kind, starts, period, width, members):
    step = panel_steps()[kind]
    for block, begin in enumerate(starts):
        span = slice(block * CHUNK, (block + 1) * CHUNK)
        out[:, span] = weight(cols[0:1, span], row_coord[...], step, begin, period, width, members)


def finish_kernel(row_coord, row_level, *refs, plan, period, width, members):
    out, scratch, sems = refs[-3], refs[-2], refs[-1]
    steps = panel_steps()
    coord, level = row_coord[...], row_level[...]
    copies = []
    at = 0
    for n, kind, starts in plan:
        cols, parts = refs[at], refs[at + 1 : at + 1 + n]
        at += 1 + n
        step = steps[kind]
        for block, begin in enumerate(starts):
            span = slice(block * CHUNK, (block + 1) * CHUNK)
            slot = len(copies)
            raw = parts[0][:, span]
            if len(parts) > 1:
                share = len(starts) // (len(parts) - 1)
                part = parts[1 + block // share]
                if part.dtype == jnp.int32:
                    raw = raw + unpack(part, block % share, raw.shape[0])
                else:
                    raw = raw + part[:, span]
            if cols.shape[0] == out.shape[0]:
                scale = cols[:, span]
            else:
                scale = weight(cols[0:1, span], coord, step, begin, period, width, members)
            c = scale * raw
            scratch[slot] = c - jnp.clip(c, -level, level)
            target = pl.multiple_of(step * width + begin, CHUNK)
            copy = pltpu.make_async_copy(scratch.at[slot], out.at[:, pl.ds(target, CHUNK)], sems.at[slot])
            copy.start()
            copies.append(copy)
    for copy in copies:
        copy.wait()


def finish(row_coord, row_level, groups, out, shape, period, width, members):
    operands = [row_coord, row_level]
    plan = []
    for cols, parts, kind, starts in groups:
        operands += [cols, *parts]
        plan.append((len(parts), kind, starts))
    copies = sum(len(starts) for _, _, starts in plan)
    specs = [VMEM] * len(operands)
    aliases = {}
    if out is not None:
        aliases = {len(operands): 0}
        operands.append(out)
        specs.append(pl.BlockSpec(memory_space=pl.ANY))
    return pl.pallas_call(
        functools.partial(finish_kernel, plan=plan, period=period, width=width, members=members),
        out_shape=jax.ShapeDtypeStruct(shape, F32),
        in_specs=specs,
        out_specs=pl.BlockSpec(memory_space=pl.ANY),
        scratch_shapes=[pltpu.VMEM((copies, shape[0], CHUNK), F32), pltpu.SemaphoreType.DMA((copies,))],
        input_output_aliases=aliases,
        compiler_params=PARAMS,
        cost_estimate=pl.CostEstimate(flops=1, bytes_accessed=1, transcendentals=0),
        name="finish",
    )(*operands)


def per_device(perturbations, node_coord, threshold_level):
    members, width = perturbations.shape
    groups = lax.axis_size("mem")
    count = lax.axis_size("mesh")
    period = 4.0 * width * count
    owned = width // groups
    everyone = members * groups
    split = groups == 2
    rows = [owned] * groups if split else [width]
    shape = (owned, 4 * width)
    coord = node_coord.reshape(1, width)
    levels = threshold_level.reshape(1, width)

    def permute(array, pairs):
        return lax.ppermute(array, "mesh", pairs)

    everywhere = range(count)
    swap_x = [(p, p ^ 2) for p in everywhere]
    relay = [(p, (p - 4) % count) for p in everywhere if p % 4 >= 2]
    back_two = [(p, (p - 2) % count) for p in everywhere]
    siblings = [(p, p ^ 1) for p in everywhere]
    extra_pairs = [(p, p - 1) if p % 2 else (p, (p - 3) % count) for p in everywhere]

    def reduced(parts):
        if split:
            return [parts[-1]] + [lax.ppermute(a, "mem", [(0, 1), (1, 0)]) for a in parts[:-1]]
        return [lax.psum_scatter(parts[0], "mem", scatter_dimension=0, tiled=True)]

    half = width // 2
    low = perturbations[:, :half]
    high, *highs = prepare(after(perturbations, low), coord)
    lt, row_coord, row_level, *own = own_tile(low, high, coord, levels, owned, rows)
    own_parts = reduced(own)
    own_cols = jnp.concatenate([high[members : members + PAD // 2], high[members + PAD // 2 :]], axis=1).astype(F32)

    first = permute(low, swap_x)
    extra = [permute(a, extra_pairs) for a in (low, high)]
    straight = [permute(after(a, first), back_two) for a in highs]
    near = cut(first)
    passed = [permute(a, relay) for a in near]

    def tile(panels, picks, *tokens, keep=False):
        return panel_tile(after(lt, *tokens), panels, picks, rows, keep)

    def finished(out, token, *groups):
        groups = [(after(groups[0][0], token), *groups[0][1:])] + list(groups[1:])
        return finish(row_coord, row_level, groups, out, shape, period, width, everyone)

    extra_cols, *extra_parts = tile(extra, [[0, 1]], own_parts[-1])
    extra_parts = reduced(extra_parts)
    whole = [i * CHUNK for i in range(width // CHUNK)]
    places = [whole[::2], whole[1::2]]
    sides = [[0, 2], [1, 2]]
    cols0, *parts0, two0 = tile([near[0], passed[0], straight[0]], sides, extra_cols, keep=True)
    parts0 = reduced(parts0)
    out = finished(None, cols0, (own_cols, own_parts, "own", whole), (extra_cols, extra_parts, "extra", whole))
    cols1, *parts1, two1 = tile([near[1], passed[1], straight[1]], sides, out, parts0[-1], keep=True)
    parts1 = reduced(parts1)
    other0, other1 = permute(two0, siblings), permute(two1, siblings)
    other_cols0, *other_parts0 = tile([other0], [[0]], cols1)
    other_parts0 = reduced(other_parts0)
    other_cols1, *other_parts1 = tile([other1], [[0]], other_cols0)
    other_parts1 = reduced(other_parts1)
    weights = call(
        functools.partial(
            weigh_kernel, kind="other", starts=places[1], period=period, width=width, members=everyone
        ),
        [jax.ShapeDtypeStruct((owned, half), F32)],
        row_coord,
        other_cols1,
        name="weigh",
    )[0]
    out = finished(
        out,
        weights,
        (cols0, parts0, "two", places[0]),
        (cols1, parts1, "two", places[1]),
        (other_cols0, other_parts0, "other", places[0]),
    )
    return finished(out, other_cols1, (weights, other_parts1, "other", places[1]))


def solution(mesh):
    in_specs = (P("mem", "mesh"), P("mesh"), P("mesh"))
    out_specs = P(("mesh", "mem"), None)
    return jax.shard_map(
        per_device, mesh=mesh, in_specs=in_specs, out_specs=out_specs, check_vma=False
    )
```

```python
import functools

import jax
import jax.numpy as jnp
from jax import lax
from jax.experimental import pallas as pl
from jax.experimental.pallas import tpu as pltpu
from jax.sharding import PartitionSpec as P

PAD = 16
TAIL = 32
STEPS = 32766.0
CHUNK = 128
PARAMS = pltpu.CompilerParams(vmem_limit_bytes=32 * 1024 * 1024)
VMEM = pl.BlockSpec(memory_space=pltpu.VMEM)
F32 = jnp.float32


def after(value, *tokens):
    return lax.optimization_barrier((value, *tokens))[0]


def call(kernel, outs, *operands, name, flops=0):
    size = sum(o.size * o.dtype.itemsize for o in (*outs, *operands))
    return pl.pallas_call(
        kernel,
        out_shape=outs,
        in_specs=[VMEM] * len(operands),
        out_specs=[VMEM] * len(outs),
        compiler_params=PARAMS,
        cost_estimate=pl.CostEstimate(flops=1, bytes_accessed=1, transcendentals=0),
        name=name,
    )(*operands)


def gc_taper(r):
    near = 1.0 + r * r * (-5.0 / 3.0 + r * (0.625 + r * (0.5 - 0.25 * r)))
    s = jnp.maximum(r, 1.0)
    far = 4.0 - 5.0 * s + s * s * (5.0 / 3.0 + s * (0.625 + s * (s * (1.0 / 12.0) - 0.5))) - (2.0 / 3.0) / s
    return jnp.where(r <= 1.0, near, jnp.where(r <= 2.0, far, 0.0))


def prepare_kernel(x, coord, high, *parts):
    members, width = x.shape
    half = width // 2
    first = 4 * width * lax.axis_index("mesh")
    jitter = coord[...] - first - 4 * lax.broadcasted_iota(jnp.int32, (1, width), 1)
    jitter = jitter.astype(F32)
    high[:members, :] = x[:, half:]
    high[members:, :] = jnp.concatenate(
        [jnp.broadcast_to(jitter[:, :half], (PAD // 2, half)), jnp.broadcast_to(jitter[:, half:], (PAD // 2, half))],
        axis=0,
    ).astype(x.dtype)
    for i, part in enumerate(parts):
        span = slice(i * CHUNK, (i + 1) * CHUNK)
        part[: members + PAD, :] = high[:, span]
        part[members + PAD :, :] = x[members - TAIL :, span]


def cut_kernel(whole, *parts):
    wide = parts[0].shape[1]
    for i, part in enumerate(parts):
        part[...] = whole[:, i * wide : (i + 1) * wide]


def cut(panel):
    half = jax.ShapeDtypeStruct((panel.shape[0], panel.shape[1] // 2), panel.dtype)
    return call(cut_kernel, [half] * 2, panel, name="cut")


def head_kernel(whole, part):
    part[...] = whole[: part.shape[0], :]


def head(panel):
    short = jax.ShapeDtypeStruct((panel.shape[0] - TAIL, panel.shape[1]), panel.dtype)
    return call(head_kernel, [short], panel, name="head")[0]


def prepare(x, coord):
    members, width = x.shape
    outs = [jax.ShapeDtypeStruct((members + PAD, width // 2), x.dtype)]
    outs += [jax.ShapeDtypeStruct((members + PAD + TAIL, CHUNK), x.dtype)] * (width // 2 // CHUNK)
    return call(prepare_kernel, outs, x, coord, name="prepare")


def own_kernel(low, high, coord, level, lt, row_coord, row_level, *outs, owned, split):
    width, members = lt.shape
    groups = width // owned
    half = width // 2
    mem = lax.axis_index("mem")
    for at, part in ((0, low), (half, high)):
        columns = part[:members, :].T
        if split:
            begin = lax.rem(mem + 1 + at // half, 2) * half
            lt[pl.ds(pl.multiple_of(begin, half), half), :] = columns
        else:
            lt[at : at + half, :] = columns
    for at, part in ((0, low), (half, high)):
        tile = jnp.dot(lt[...], part[:members, :], preferred_element_type=F32)
        store_rows(tile, outs, at)
    rows = jnp.concatenate(
        [jnp.broadcast_to(coord[...], (CHUNK, width)), jnp.broadcast_to(level[...], (CHUNK, width))], axis=0
    )
    rows = rows.astype(F32)
    for part in range(groups):

        @pl.when(mem == part)
        def _():
            span = slice(part * owned, (part + 1) * owned)
            row_coord[...] = rows[:CHUNK, span].T
            row_level[...] = 0.05 * rows[CHUNK:, span].T


def store_rows(tile, outs, at):
    first = 0
    for out in outs:
        out[:, at : at + tile.shape[1]] = tile[first : first + out.shape[0]]
        first += out.shape[0]


def own_tile(low, high, coord, level, owned, rows):
    members, width = low.shape[0], 2 * low.shape[1]
    return call(
        functools.partial(own_kernel, owned=owned, split=len(rows) > 1),
        [jax.ShapeDtypeStruct((width, members), low.dtype)]
        + [jax.ShapeDtypeStruct((owned, CHUNK), F32)] * 2
        + [jax.ShapeDtypeStruct((r, width), F32) for r in rows],
        low,
        high,
        coord,
        level,
        name="own_tile",
        flops=2 * members * width * width,
    )


def narrowed(block):
    top = jnp.maximum(jnp.max(jnp.abs(block), axis=0, keepdims=True), 2.0**-126)
    power = jnp.ceil(8.0 * jnp.log2(top) + 0.01)
    steps = jnp.round(block * jnp.exp2(-0.125 * power) * STEPS)
    return steps.astype(jnp.int32), power.astype(jnp.int32)


def widened(steps, power):
    return (steps.astype(F32) * jnp.exp2(0.125 * power.astype(F32) - 16.0)) * (65536.0 / STEPS)


def pack(tile, packed):
    rows = tile.shape[0]
    for at in range(0, tile.shape[1] // 2, CHUNK):
        span = slice(at, at + CHUNK)
        high, high_power = narrowed(tile[:, 2 * at : 2 * at + CHUNK])
        low, low_power = narrowed(tile[:, 2 * at + CHUNK : 2 * at + 2 * CHUNK])
        packed[:rows, span] = (high << 16) | (low & 0xFFFF)
        packed[rows : rows + 4, span] = jnp.broadcast_to(high_power, (4, CHUNK))
        packed[rows + 4 :, span] = jnp.broadcast_to(low_power, (4, CHUNK))


def unpack(packed, block, rows):
    span = slice((block // 2) * CHUNK, (block // 2 + 1) * CHUNK)
    words = packed[:rows, span]
    if block % 2 == 0:
        return widened(words >> 16, packed[rows : rows + 1, span])
    return widened((words << 16) >> 16, packed[rows + 4 : rows + 5, span])


def panel_kernel(lt, *refs, picks, count, rows, keep):
    panels, cols, outs = refs[:count], refs[count], refs[count + 1 :]
    members = lt.shape[1]

    def run(which):
        chosen = [panels[i] for i in which]
        half = cols.shape[1] // 2
        pad = [chosen[-1][members : members + PAD, :].astype(F32)] * 2
        if len(chosen) == 1:
            pad = [pad[0][:, :half], pad[0][:, half:]]
        cols[:, :half] = pad[0][: PAD // 2]
        cols[:, half:] = pad[1][PAD // 2 :]
        blocks = [panel[:members, :] for panel in chosen]
        if chosen[0].shape[0] < members:
            blocks[0] = jnp.concatenate([chosen[0][...], chosen[1][members + PAD :, :]], axis=0)
        if keep:
            for at, block in zip((0, half), blocks):
                outs[-1][:members, at : at + half] = block
                outs[-1][members:, at : at + half] = chosen[-1][members : members + PAD, :]
        block = jnp.concatenate(blocks, axis=1)
        tile = jnp.dot(lt[...], block, preferred_element_type=F32)
        if len(rows) > 1:
            pack(tile[: rows[0]], outs[0])
            outs[1][...] = tile[rows[0] :]
        else:
            outs[0][...] = tile

    if len(picks) == 1:
        run(picks[0])
    else:
        cross = lax.rem(lax.axis_index("mesh") // 2, 2)
        for value, which in enumerate(picks):
            pl.when(cross == value)(functools.partial(run, which))


def panel_tile(lt, panels, picks, rows, keep=False):
    wide = sum(panels[i].shape[1] for i in picks[0])
    width, members = lt.shape
    return call(
        functools.partial(panel_kernel, picks=picks, count=len(panels), rows=rows, keep=keep),
        [jax.ShapeDtypeStruct((8, wide), F32)]
        + ([jax.ShapeDtypeStruct((rows[0] + 8, wide // 2), jnp.int32)] if len(rows) > 1 else [])
        + [jax.ShapeDtypeStruct((rows[-1], wide), F32)]
        + ([jax.ShapeDtypeStruct((members + PAD, wide), lt.dtype)] if keep else []),
        lt,
        *panels,
        name="panel_tile",
    )


def panel_steps():
    odd = lax.rem(lax.axis_index("mesh"), 2)
    return {"own": 0, "two": 2, "extra": 1 + 2 * odd, "other": 3 - 2 * odd}


def weight(offsets, row_coord, step, first, period, width, members):
    panel = lax.rem(lax.axis_index("mesh") + step, lax.axis_size("mesh"))
    base = (4 * (panel * width + first)).astype(F32)
    place = 4 * lax.broadcasted_iota(jnp.int32, (1, CHUNK), 1)
    gap = jnp.abs(offsets + (base + place.astype(F32)) - row_coord)
    dist = jnp.minimum(gap, period - gap)
    return gc_taper(dist * (1.0 / (12 * width))) * (1.0 / (members - 1))


def weigh_kernel(row_coord, cols, out, *, kind, starts, period, width, members):
    step = panel_steps()[kind]
    for block, begin in enumerate(starts):
        span = slice(block * CHUNK, (block + 1) * CHUNK)
        out[:, span] = weight(cols[0:1, span], row_coord[...], step, begin, period, width, members)


def finish_kernel(row_coord, row_level, *refs, plan, period, width, members):
    out, scratch, sems = refs[-3], refs[-2], refs[-1]
    steps = panel_steps()
    coord, level = row_coord[...], row_level[...]
    copies = []
    at = 0
    for n, kind, starts in plan:
        cols, parts = refs[at], refs[at + 1 : at + 1 + n]
        at += 1 + n
        step = steps[kind]
        for block, begin in enumerate(starts):
            span = slice(block * CHUNK, (block + 1) * CHUNK)
            slot = len(copies)
            raw = parts[0][:, span]
            if len(parts) > 1:
                share = len(starts) // (len(parts) - 1)
                part = parts[1 + block // share]
                if part.dtype == jnp.int32:
                    raw = raw + unpack(part, block % share, raw.shape[0])
                else:
                    raw = raw + part[:, span]
            if cols.shape[0] == out.shape[0]:
                scale = cols[:, span]
            else:
                scale = weight(cols[0:1, span], coord, step, begin, period, width, members)
            c = scale * raw
            scratch[slot] = c - jnp.clip(c, -level, level)
            target = pl.multiple_of(step * width + begin, CHUNK)
            copy = pltpu.make_async_copy(scratch.at[slot], out.at[:, pl.ds(target, CHUNK)], sems.at[slot])
            copy.start()
            copies.append(copy)
    for copy in copies:
        copy.wait()


def finish(row_coord, row_level, groups, out, shape, period, width, members):
    operands = [row_coord, row_level]
    plan = []
    for cols, parts, kind, starts in groups:
        operands += [cols, *parts]
        plan.append((len(parts), kind, starts))
    copies = sum(len(starts) for _, _, starts in plan)
    specs = [VMEM] * len(operands)
    aliases = {}
    if out is not None:
        aliases = {len(operands): 0}
        operands.append(out)
        specs.append(pl.BlockSpec(memory_space=pl.ANY))
    return pl.pallas_call(
        functools.partial(finish_kernel, plan=plan, period=period, width=width, members=members),
        out_shape=jax.ShapeDtypeStruct(shape, F32),
        in_specs=specs,
        out_specs=pl.BlockSpec(memory_space=pl.ANY),
        scratch_shapes=[pltpu.VMEM((copies, shape[0], CHUNK), F32), pltpu.SemaphoreType.DMA((copies,))],
        input_output_aliases=aliases,
        compiler_params=PARAMS,
        cost_estimate=pl.CostEstimate(flops=1, bytes_accessed=1, transcendentals=0),
        name="finish",
    )(*operands)


def per_device(perturbations, node_coord, threshold_level):
    members, width = perturbations.shape
    groups = lax.axis_size("mem")
    count = lax.axis_size("mesh")
    period = 4.0 * width * count
    owned = width // groups
    everyone = members * groups
    split = groups == 2
    rows = [owned] * groups if split else [width]
    shape = (owned, 4 * width)
    coord = node_coord.reshape(1, width)
    levels = threshold_level.reshape(1, width)

    def permute(array, pairs):
        return lax.ppermute(array, "mesh", pairs)

    everywhere = range(count)
    swap_x = [(p, p ^ 2) for p in everywhere]
    relay = [(p, (p - 4) % count) for p in everywhere if p % 4 >= 2]
    back_two = [(p, (p - 2) % count) for p in everywhere]
    siblings = [(p, p ^ 1) for p in everywhere]
    extra_pairs = [(p, p - 1) if p % 2 else (p, (p - 3) % count) for p in everywhere]

    def reduced(parts):
        if split:
            return [parts[-1]] + [lax.ppermute(a, "mem", [(0, 1), (1, 0)]) for a in parts[:-1]]
        return [lax.psum_scatter(parts[0], "mem", scatter_dimension=0, tiled=True)]

    half = width // 2
    low = perturbations[:, :half]
    high, *highs = prepare(after(perturbations, low), coord)
    lt, row_coord, row_level, *own = own_tile(low, high, coord, levels, owned, rows)
    own_parts = reduced(own)
    own_cols = jnp.concatenate([high[members : members + PAD // 2], high[members + PAD // 2 :]], axis=1).astype(F32)

    first = permute(head(low), swap_x)
    extra = [permute(a, extra_pairs) for a in (low, high)]
    straight = [permute(after(a, first), back_two) for a in highs]
    near = cut(first)
    passed = [permute(a, relay) for a in near]

    def tile(panels, picks, *tokens, keep=False):
        return panel_tile(after(lt, *tokens), panels, picks, rows, keep)

    def finished(out, token, *groups):
        groups = [(after(groups[0][0], token), *groups[0][1:])] + list(groups[1:])
        return finish(row_coord, row_level, groups, out, shape, period, width, everyone)

    extra_cols, *extra_parts = tile(extra, [[0, 1]], own_parts[-1])
    extra_parts = reduced(extra_parts)
    whole = [i * CHUNK for i in range(width // CHUNK)]
    places = [whole[::2], whole[1::2]]
    sides = [[0, 2], [1, 2]]
    cols0, *parts0, two0 = tile([near[0], passed[0], straight[0]], sides, extra_cols, keep=True)
    parts0 = reduced(parts0)
    out = finished(None, cols0, (own_cols, own_parts, "own", whole), (extra_cols, extra_parts, "extra", whole))
    cols1, *parts1, two1 = tile([near[1], passed[1], straight[1]], sides, out, parts0[-1], keep=True)
    parts1 = reduced(parts1)
    other0, other1 = permute(two0, siblings), permute(two1, siblings)
    other_cols0, *other_parts0 = tile([other0], [[0]], cols1)
    other_parts0 = reduced(other_parts0)
    other_cols1, *other_parts1 = tile([other1], [[0]], other_cols0)
    other_parts1 = reduced(other_parts1)
    weights = call(
        functools.partial(
            weigh_kernel, kind="other", starts=places[1], period=period, width=width, members=everyone
        ),
        [jax.ShapeDtypeStruct((owned, half), F32)],
        row_coord,
        other_cols1,
        name="weigh",
    )[0]
    out = finished(
        out,
        weights,
        (cols0, parts0, "two", places[0]),
        (cols1, parts1, "two", places[1]),
        (other_cols0, other_parts0, "other", places[0]),
    )
    return finished(out, other_cols1, (weights, other_parts1, "other", places[1]))


def solution(mesh):
    in_specs = (P("mem", "mesh"), P("mesh"), P("mesh"))
    out_specs = P(("mesh", "mem"), None)
    return jax.shard_map(
        per_device, mesh=mesh, in_specs=in_specs, out_specs=out_specs, check_vma=False
    )
```

```python
import functools

import jax
import jax.numpy as jnp
from jax import lax
from jax.experimental import pallas as pl
from jax.experimental.pallas import tpu as pltpu
from jax.sharding import PartitionSpec as P

PAD = 16
TAIL = 32
STEPS = 32766.0
CHUNK = 128
PARAMS = pltpu.CompilerParams(vmem_limit_bytes=32 * 1024 * 1024)
VMEM = pl.BlockSpec(memory_space=pltpu.VMEM)
F32 = jnp.float32


def after(value, *tokens):
    return lax.optimization_barrier((value, *tokens))[0]


def call(kernel, outs, *operands, name, flops=0):
    size = sum(o.size * o.dtype.itemsize for o in (*outs, *operands))
    return pl.pallas_call(
        kernel,
        out_shape=outs,
        in_specs=[VMEM] * len(operands),
        out_specs=[VMEM] * len(outs),
        compiler_params=PARAMS,
        cost_estimate=pl.CostEstimate(flops=1, bytes_accessed=1, transcendentals=0),
        name=name,
    )(*operands)


def gc_taper(r):
    near = 1.0 + r * r * (-5.0 / 3.0 + r * (0.625 + r * (0.5 - 0.25 * r)))
    s = jnp.maximum(r, 1.0)
    far = 4.0 - 5.0 * s + s * s * (5.0 / 3.0 + s * (0.625 + s * (s * (1.0 / 12.0) - 0.5))) - (2.0 / 3.0) / s
    return jnp.where(r <= 1.0, near, jnp.where(r <= 2.0, far, 0.0))


def prepare_kernel(x, coord, high, *parts):
    members, width = x.shape
    half = width // 2
    first = 4 * width * lax.axis_index("mesh")
    jitter = coord[...] - first - 4 * lax.broadcasted_iota(jnp.int32, (1, width), 1)
    jitter = jitter.astype(F32)
    high[:members, :] = x[:, half:]
    high[members:, :] = jnp.concatenate(
        [jnp.broadcast_to(jitter[:, :half], (PAD // 2, half)), jnp.broadcast_to(jitter[:, half:], (PAD // 2, half))],
        axis=0,
    ).astype(x.dtype)
    for i, part in enumerate(parts):
        span = slice(i * CHUNK, (i + 1) * CHUNK)
        part[: members + PAD, :] = high[:, span]
        part[members + PAD :, :] = x[members - TAIL :, span]


def cut_kernel(whole, *parts):
    wide = parts[0].shape[1]
    for i, part in enumerate(parts):
        part[...] = whole[:, i * wide : (i + 1) * wide]


def cut(panel):
    half = jax.ShapeDtypeStruct((panel.shape[0], panel.shape[1] // 2), panel.dtype)
    return call(cut_kernel, [half] * 2, panel, name="cut")


def head_kernel(whole, part):
    part[...] = whole[: part.shape[0], :]


def head(panel):
    short = jax.ShapeDtypeStruct((panel.shape[0] - TAIL, panel.shape[1]), panel.dtype)
    return call(head_kernel, [short], panel, name="head")[0]


def prepare(x, coord):
    members, width = x.shape
    outs = [jax.ShapeDtypeStruct((members + PAD, width // 2), x.dtype)]
    outs += [jax.ShapeDtypeStruct((members + PAD + TAIL, CHUNK), x.dtype)] * (width // 2 // CHUNK)
    return call(prepare_kernel, outs, x, coord, name="prepare")


def own_kernel(low, high, coord, level, lt, row_coord, row_level, *outs, owned, split):
    width, members = lt.shape
    groups = width // owned
    half = width // 2
    mem = lax.axis_index("mem")
    for at, part in ((0, low), (half, high)):
        columns = part[:members, :].T
        if split:
            begin = lax.rem(mem + 1 + at // half, 2) * half
            lt[pl.ds(pl.multiple_of(begin, half), half), :] = columns
        else:
            lt[at : at + half, :] = columns
    for at, part in ((0, low), (half, high)):
        tile = jnp.dot(lt[...], part[:members, :], preferred_element_type=F32)
        store_rows(tile, outs, at)
    rows = jnp.concatenate(
        [jnp.broadcast_to(coord[...], (CHUNK, width)), jnp.broadcast_to(level[...], (CHUNK, width))], axis=0
    )
    rows = rows.astype(F32)
    for part in range(groups):

        @pl.when(mem == part)
        def _():
            span = slice(part * owned, (part + 1) * owned)
            row_coord[...] = rows[:CHUNK, span].T
            row_level[...] = 0.05 * rows[CHUNK:, span].T


def store_rows(tile, outs, at):
    first = 0
    for out in outs:
        out[:, at : at + tile.shape[1]] = tile[first : first + out.shape[0]]
        first += out.shape[0]


def own_tile(low, high, coord, level, owned, rows):
    members, width = low.shape[0], 2 * low.shape[1]
    return call(
        functools.partial(own_kernel, owned=owned, split=len(rows) > 1),
        [jax.ShapeDtypeStruct((width, members), low.dtype)]
        + [jax.ShapeDtypeStruct((owned, CHUNK), F32)] * 2
        + [jax.ShapeDtypeStruct((r, width), F32) for r in rows],
        low,
        high,
        coord,
        level,
        name="own_tile",
        flops=2 * members * width * width,
    )


def narrowed(block):
    top = jnp.maximum(jnp.max(jnp.abs(block), axis=0, keepdims=True), 2.0**-126)
    power = jnp.ceil(8.0 * jnp.log2(top) + 0.01)
    root = jnp.exp2(-0.0625 * power)
    steps = jnp.round((block * root) * (root * STEPS))
    return steps.astype(jnp.int32), power.astype(jnp.int32)


def widened(steps, power):
    root = jnp.exp2(0.0625 * power.astype(F32))
    return (steps.astype(F32) * (root * (1.0 / STEPS))) * root


def pack(tile, packed):
    rows = tile.shape[0]
    for at in range(0, tile.shape[1] // 2, CHUNK):
        span = slice(at, at + CHUNK)
        high, high_power = narrowed(tile[:, 2 * at : 2 * at + CHUNK])
        low, low_power = narrowed(tile[:, 2 * at + CHUNK : 2 * at + 2 * CHUNK])
        packed[:rows, span] = (high << 16) | (low & 0xFFFF)
        packed[rows : rows + 4, span] = jnp.broadcast_to(high_power, (4, CHUNK))
        packed[rows + 4 :, span] = jnp.broadcast_to(low_power, (4, CHUNK))


def unpack(packed, block, rows):
    span = slice((block // 2) * CHUNK, (block // 2 + 1) * CHUNK)
    words = packed[:rows, span]
    if block % 2 == 0:
        return widened(words >> 16, packed[rows : rows + 1, span])
    return widened((words << 16) >> 16, packed[rows + 4 : rows + 5, span])


def panel_kernel(lt, *refs, picks, count, rows, keep):
    panels, cols, outs = refs[:count], refs[count], refs[count + 1 :]
    members = lt.shape[1]

    def run(which):
        chosen = [panels[i] for i in which]
        half = cols.shape[1] // 2
        pad = [chosen[-1][members : members + PAD, :].astype(F32)] * 2
        if len(chosen) == 1:
            pad = [pad[0][:, :half], pad[0][:, half:]]
        cols[:, :half] = pad[0][: PAD // 2]
        cols[:, half:] = pad[1][PAD // 2 :]
        blocks = [panel[:members, :] for panel in chosen]
        if chosen[0].shape[0] < members:
            blocks[0] = jnp.concatenate([chosen[0][...], chosen[1][members + PAD :, :]], axis=0)
        if keep:
            for at, block in zip((0, half), blocks):
                outs[-1][:members, at : at + half] = block
                outs[-1][members:, at : at + half] = chosen[-1][members : members + PAD, :]
        block = jnp.concatenate(blocks, axis=1)
        tile = jnp.dot(lt[...], block, preferred_element_type=F32)
        if len(rows) > 1:
            pack(tile[: rows[0]], outs[0])
            outs[1][...] = tile[rows[0] :]
        else:
            outs[0][...] = tile

    if len(picks) == 1:
        run(picks[0])
    else:
        cross = lax.rem(lax.axis_index("mesh") // 2, 2)
        for value, which in enumerate(picks):
            pl.when(cross == value)(functools.partial(run, which))


def panel_tile(lt, panels, picks, rows, keep=False):
    wide = sum(panels[i].shape[1] for i in picks[0])
    width, members = lt.shape
    return call(
        functools.partial(panel_kernel, picks=picks, count=len(panels), rows=rows, keep=keep),
        [jax.ShapeDtypeStruct((8, wide), F32)]
        + ([jax.ShapeDtypeStruct((rows[0] + 8, wide // 2), jnp.int32)] if len(rows) > 1 else [])
        + [jax.ShapeDtypeStruct((rows[-1], wide), F32)]
        + ([jax.ShapeDtypeStruct((members + PAD, wide), lt.dtype)] if keep else []),
        lt,
        *panels,
        name="panel_tile",
    )


def panel_steps():
    odd = lax.rem(lax.axis_index("mesh"), 2)
    return {"own": 0, "two": 2, "extra": 1 + 2 * odd, "other": 3 - 2 * odd}


def weight(offsets, row_coord, step, first, period, width, members):
    panel = lax.rem(lax.axis_index("mesh") + step, lax.axis_size("mesh"))
    base = (4 * (panel * width + first)).astype(F32)
    place = 4 * lax.broadcasted_iota(jnp.int32, (1, CHUNK), 1)
    gap = jnp.abs(offsets + (base + place.astype(F32)) - row_coord)
    dist = jnp.minimum(gap, period - gap)
    return gc_taper(dist * (1.0 / (12 * width))) * (1.0 / (members - 1))


def weigh_kernel(row_coord, cols, out, *, kind, starts, period, width, members):
    step = panel_steps()[kind]
    for block, begin in enumerate(starts):
        span = slice(block * CHUNK, (block + 1) * CHUNK)
        out[:, span] = weight(cols[0:1, span], row_coord[...], step, begin, period, width, members)


def finish_kernel(row_coord, row_level, *refs, plan, period, width, members):
    out, scratch, sems = refs[-3], refs[-2], refs[-1]
    steps = panel_steps()
    coord, level = row_coord[...], row_level[...]
    copies = []
    at = 0
    for n, kind, starts in plan:
        cols, parts = refs[at], refs[at + 1 : at + 1 + n]
        at += 1 + n
        step = steps[kind]
        for block, begin in enumerate(starts):
            span = slice(block * CHUNK, (block + 1) * CHUNK)
            slot = len(copies)
            raw = parts[0][:, span]
            if len(parts) > 1:
                share = len(starts) // (len(parts) - 1)
                part = parts[1 + block // share]
                if part.dtype == jnp.int32:
                    raw = raw + unpack(part, block % share, raw.shape[0])
                else:
                    raw = raw + part[:, span]
            if cols.shape[0] == out.shape[0]:
                scale = cols[:, span]
            else:
                scale = weight(cols[0:1, span], coord, step, begin, period, width, members)
            c = scale * raw
            scratch[slot] = c - jnp.clip(c, -level, level)
            target = pl.multiple_of(step * width + begin, CHUNK)
            copy = pltpu.make_async_copy(scratch.at[slot], out.at[:, pl.ds(target, CHUNK)], sems.at[slot])
            copy.start()
            copies.append(copy)
    for copy in copies:
        copy.wait()


def finish(row_coord, row_level, groups, out, shape, period, width, members):
    operands = [row_coord, row_level]
    plan = []
    for cols, parts, kind, starts in groups:
        operands += [cols, *parts]
        plan.append((len(parts), kind, starts))
    copies = sum(len(starts) for _, _, starts in plan)
    specs = [VMEM] * len(operands)
    aliases = {}
    if out is not None:
        aliases = {len(operands): 0}
        operands.append(out)
        specs.append(pl.BlockSpec(memory_space=pl.ANY))
    return pl.pallas_call(
        functools.partial(finish_kernel, plan=plan, period=period, width=width, members=members),
        out_shape=jax.ShapeDtypeStruct(shape, F32),
        in_specs=specs,
        out_specs=pl.BlockSpec(memory_space=pl.ANY),
        scratch_shapes=[pltpu.VMEM((copies, shape[0], CHUNK), F32), pltpu.SemaphoreType.DMA((copies,))],
        input_output_aliases=aliases,
        compiler_params=PARAMS,
        cost_estimate=pl.CostEstimate(flops=1, bytes_accessed=1, transcendentals=0),
        name="finish",
    )(*operands)


def per_device(perturbations, node_coord, threshold_level):
    members, width = perturbations.shape
    groups = lax.axis_size("mem")
    count = lax.axis_size("mesh")
    period = 4.0 * width * count
    owned = width // groups
    everyone = members * groups
    split = groups == 2
    rows = [owned] * groups if split else [width]
    shape = (owned, 4 * width)
    coord = node_coord.reshape(1, width)
    levels = threshold_level.reshape(1, width)

    def permute(array, pairs):
        return lax.ppermute(array, "mesh", pairs)

    everywhere = range(count)
    swap_x = [(p, p ^ 2) for p in everywhere]
    relay = [(p, (p - 4) % count) for p in everywhere if p % 4 >= 2]
    back_two = [(p, (p - 2) % count) for p in everywhere]
    siblings = [(p, p ^ 1) for p in everywhere]
    extra_pairs = [(p, p - 1) if p % 2 else (p, (p - 3) % count) for p in everywhere]

    def reduced(parts):
        if split:
            return [parts[-1]] + [lax.ppermute(a, "mem", [(0, 1), (1, 0)]) for a in parts[:-1]]
        return [lax.psum_scatter(parts[0], "mem", scatter_dimension=0, tiled=True)]

    half = width // 2
    low = perturbations[:, :half]
    high, *highs = prepare(after(perturbations, low), coord)
    lt, row_coord, row_level, *own = own_tile(low, high, coord, levels, owned, rows)
    own_parts = reduced(own)
    own_cols = jnp.concatenate([high[members : members + PAD // 2], high[members + PAD // 2 :]], axis=1).astype(F32)

    first = permute(head(low), swap_x)
    extra = [permute(a, extra_pairs) for a in (low, high)]
    straight = [permute(after(a, first), back_two) for a in highs]
    near = cut(first)
    passed = [permute(a, relay) for a in near]

    def tile(panels, picks, *tokens, keep=False):
        return panel_tile(after(lt, *tokens), panels, picks, rows, keep)

    def finished(out, token, *groups):
        groups = [(after(groups[0][0], token), *groups[0][1:])] + list(groups[1:])
        return finish(row_coord, row_level, groups, out, shape, period, width, everyone)

    extra_cols, *extra_parts = tile(extra, [[0, 1]], own_parts[-1])
    extra_parts = reduced(extra_parts)
    whole = [i * CHUNK for i in range(width // CHUNK)]
    places = [whole[::2], whole[1::2]]
    sides = [[0, 2], [1, 2]]
    cols0, *parts0, two0 = tile([near[0], passed[0], straight[0]], sides, extra_cols, keep=True)
    parts0 = reduced(parts0)
    out = finished(None, cols0, (own_cols, own_parts, "own", whole), (extra_cols, extra_parts, "extra", whole))
    cols1, *parts1, two1 = tile([near[1], passed[1], straight[1]], sides, out, parts0[-1], keep=True)
    parts1 = reduced(parts1)
    other0, other1 = permute(two0, siblings), permute(two1, siblings)
    other_cols0, *other_parts0 = tile([other0], [[0]], cols1)
    other_parts0 = reduced(other_parts0)
    other_cols1, *other_parts1 = tile([other1], [[0]], other_cols0)
    other_parts1 = reduced(other_parts1)
    weights = call(
        functools.partial(
            weigh_kernel, kind="other", starts=places[1], period=period, width=width, members=everyone
        ),
        [jax.ShapeDtypeStruct((owned, half), F32)],
        row_coord,
        other_cols1,
        name="weigh",
    )[0]
    out = finished(
        out,
        weights,
        (cols0, parts0, "two", places[0]),
        (cols1, parts1, "two", places[1]),
        (other_cols0, other_parts0, "other", places[0]),
    )
    return finished(out, other_cols1, (weights, other_parts1, "other", places[1]))


def solution(mesh):
    in_specs = (P("mem", "mesh"), P("mesh"), P("mesh"))
    out_specs = P(("mesh", "mem"), None)
    return jax.shard_map(
        per_device, mesh=mesh, in_specs=in_specs, out_specs=out_specs, check_vma=False
    )
```

```python
import functools

import jax
import jax.numpy as jnp
from jax import lax
from jax.experimental import pallas as pl
from jax.experimental.pallas import tpu as pltpu
from jax.sharding import PartitionSpec as P

PAD = 16
TAIL = 32
STEPS = 32766.0
CHUNK = 128
PARAMS = pltpu.CompilerParams(vmem_limit_bytes=32 * 1024 * 1024)
VMEM = pl.BlockSpec(memory_space=pltpu.VMEM)
F32 = jnp.float32


def after(value, *tokens):
    return lax.optimization_barrier((value, *tokens))[0]


def call(kernel, outs, *operands, name, flops=0):
    size = sum(o.size * o.dtype.itemsize for o in (*outs, *operands))
    return pl.pallas_call(
        kernel,
        out_shape=outs,
        in_specs=[VMEM] * len(operands),
        out_specs=[VMEM] * len(outs),
        compiler_params=PARAMS,
        cost_estimate=pl.CostEstimate(flops=1, bytes_accessed=1, transcendentals=0),
        name=name,
    )(*operands)


def gc_taper(r):
    near = 1.0 + r * r * (-5.0 / 3.0 + r * (0.625 + r * (0.5 - 0.25 * r)))
    s = jnp.maximum(r, 1.0)
    far = 4.0 - 5.0 * s + s * s * (5.0 / 3.0 + s * (0.625 + s * (s * (1.0 / 12.0) - 0.5))) - (2.0 / 3.0) / s
    return jnp.where(r <= 1.0, near, jnp.where(r <= 2.0, far, 0.0))


def prepare_kernel(x, tail, coord, high, *parts):
    members, half = x.shape
    width = 2 * half
    first = 4 * width * lax.axis_index("mesh")
    jitter = coord[...] - first - 4 * lax.broadcasted_iota(jnp.int32, (1, width), 1)
    jitter = jitter.astype(F32)
    high[:members, :] = x[...]
    high[members:, :] = jnp.concatenate(
        [jnp.broadcast_to(jitter[:, :half], (PAD // 2, half)), jnp.broadcast_to(jitter[:, half:], (PAD // 2, half))],
        axis=0,
    ).astype(x.dtype)
    for i, part in enumerate(parts):
        span = slice(i * CHUNK, (i + 1) * CHUNK)
        part[: members + PAD, :] = high[:, span]
        part[members + PAD :, :] = tail[:, span]


def cut_kernel(whole, *parts):
    wide = parts[0].shape[1]
    for i, part in enumerate(parts):
        part[...] = whole[:, i * wide : (i + 1) * wide]


def cut(panel):
    half = jax.ShapeDtypeStruct((panel.shape[0], panel.shape[1] // 2), panel.dtype)
    return call(cut_kernel, [half] * 2, panel, name="cut")


def head_kernel(whole, part):
    part[...] = whole[: part.shape[0], :]


def head(panel):
    short = jax.ShapeDtypeStruct((panel.shape[0] - TAIL, panel.shape[1]), panel.dtype)
    return call(head_kernel, [short], panel, name="head")[0]


def prepare(x, tail, coord):
    members, half = x.shape
    outs = [jax.ShapeDtypeStruct((members + PAD, half), x.dtype)]
    outs += [jax.ShapeDtypeStruct((members + PAD + TAIL, CHUNK), x.dtype)] * (half // CHUNK)
    return call(prepare_kernel, outs, x, tail, coord, name="prepare")


def own_kernel(low, high, coord, level, lt, row_coord, row_level, *outs, owned, split):
    width, members = lt.shape
    groups = width // owned
    half = width // 2
    mem = lax.axis_index("mem")
    for at, part in ((0, low), (half, high)):
        columns = part[:members, :].T
        if split:
            begin = lax.rem(mem + 1 + at // half, 2) * half
            lt[pl.ds(pl.multiple_of(begin, half), half), :] = columns
        else:
            lt[at : at + half, :] = columns
    for at, part in ((0, low), (half, high)):
        tile = jnp.dot(lt[...], part[:members, :], preferred_element_type=F32)
        store_rows(tile, outs, at)
    rows = jnp.concatenate(
        [jnp.broadcast_to(coord[...], (CHUNK, width)), jnp.broadcast_to(level[...], (CHUNK, width))], axis=0
    )
    rows = rows.astype(F32)
    for part in range(groups):

        @pl.when(mem == part)
        def _():
            span = slice(part * owned, (part + 1) * owned)
            row_coord[...] = rows[:CHUNK, span].T
            row_level[...] = 0.05 * rows[CHUNK:, span].T


def store_rows(tile, outs, at):
    first = 0
    for out in outs:
        out[:, at : at + tile.shape[1]] = tile[first : first + out.shape[0]]
        first += out.shape[0]


def own_tile(low, high, coord, level, owned, rows):
    members, width = low.shape[0], 2 * low.shape[1]
    return call(
        functools.partial(own_kernel, owned=owned, split=len(rows) > 1),
        [jax.ShapeDtypeStruct((width, members), low.dtype)]
        + [jax.ShapeDtypeStruct((owned, CHUNK), F32)] * 2
        + [jax.ShapeDtypeStruct((r, width), F32) for r in rows],
        low,
        high,
        coord,
        level,
        name="own_tile",
        flops=2 * members * width * width,
    )


def narrowed(block):
    top = jnp.maximum(jnp.max(jnp.abs(block), axis=0, keepdims=True), 2.0**-126)
    power = jnp.ceil(8.0 * jnp.log2(top) + 0.01)
    root = jnp.exp2(-0.0625 * power)
    steps = jnp.round((block * root) * (root * STEPS))
    return steps.astype(jnp.int32), power.astype(jnp.int32)


def widened(steps, power):
    root = jnp.exp2(0.0625 * power.astype(F32))
    return (steps.astype(F32) * (root * (1.0 / STEPS))) * root


def pack(tile, packed):
    rows = tile.shape[0]
    for at in range(0, tile.shape[1] // 2, CHUNK):
        span = slice(at, at + CHUNK)
        high, high_power = narrowed(tile[:, 2 * at : 2 * at + CHUNK])
        low, low_power = narrowed(tile[:, 2 * at + CHUNK : 2 * at + 2 * CHUNK])
        packed[:rows, span] = (high << 16) | (low & 0xFFFF)
        packed[rows : rows + 4, span] = jnp.broadcast_to(high_power, (4, CHUNK))
        packed[rows + 4 :, span] = jnp.broadcast_to(low_power, (4, CHUNK))


def unpack(packed, block, rows):
    span = slice((block // 2) * CHUNK, (block // 2 + 1) * CHUNK)
    words = packed[:rows, span]
    if block % 2 == 0:
        return widened(words >> 16, packed[rows : rows + 1, span])
    return widened((words << 16) >> 16, packed[rows + 4 : rows + 5, span])


def panel_kernel(lt, *refs, picks, count, rows, keep):
    panels, cols, outs = refs[:count], refs[count], refs[count + 1 :]
    members = lt.shape[1]

    def run(which):
        chosen = [panels[i] for i in which]
        half = cols.shape[1] // 2
        pad = [chosen[-1][members : members + PAD, :].astype(F32)] * 2
        if len(chosen) == 1:
            pad = [pad[0][:, :half], pad[0][:, half:]]
        cols[:, :half] = pad[0][: PAD // 2]
        cols[:, half:] = pad[1][PAD // 2 :]
        blocks = [panel[:members, :] for panel in chosen]
        if chosen[0].shape[0] < members:
            blocks[0] = jnp.concatenate([chosen[0][...], chosen[1][members + PAD :, :]], axis=0)
        if keep:
            for at, block in zip((0, half), blocks):
                outs[-1][:members, at : at + half] = block
                outs[-1][members:, at : at + half] = chosen[-1][members : members + PAD, :]
        block = jnp.concatenate(blocks, axis=1)
        tile = jnp.dot(lt[...], block, preferred_element_type=F32)
        if len(rows) > 1:
            pack(tile[: rows[0]], outs[0])
            outs[1][...] = tile[rows[0] :]
        else:
            outs[0][...] = tile

    if len(picks) == 1:
        run(picks[0])
    else:
        cross = lax.rem(lax.axis_index("mesh") // 2, 2)
        for value, which in enumerate(picks):
            pl.when(cross == value)(functools.partial(run, which))


def panel_tile(lt, panels, picks, rows, keep=False):
    wide = sum(panels[i].shape[1] for i in picks[0])
    width, members = lt.shape
    return call(
        functools.partial(panel_kernel, picks=picks, count=len(panels), rows=rows, keep=keep),
        [jax.ShapeDtypeStruct((8, wide), F32)]
        + ([jax.ShapeDtypeStruct((rows[0] + 8, wide // 2), jnp.int32)] if len(rows) > 1 else [])
        + [jax.ShapeDtypeStruct((rows[-1], wide), F32)]
        + ([jax.ShapeDtypeStruct((members + PAD, wide), lt.dtype)] if keep else []),
        lt,
        *panels,
        name="panel_tile",
    )


def panel_steps():
    odd = lax.rem(lax.axis_index("mesh"), 2)
    return {"own": 0, "two": 2, "extra": 1 + 2 * odd, "other": 3 - 2 * odd}


def weight(offsets, row_coord, step, first, period, width, members):
    panel = lax.rem(lax.axis_index("mesh") + step, lax.axis_size("mesh"))
    base = (4 * (panel * width + first)).astype(F32)
    place = 4 * lax.broadcasted_iota(jnp.int32, (1, CHUNK), 1)
    gap = jnp.abs(offsets + (base + place.astype(F32)) - row_coord)
    dist = jnp.minimum(gap, period - gap)
    return gc_taper(dist * (1.0 / (12 * width))) * (1.0 / (members - 1))


def weigh_kernel(row_coord, cols, out, *, kind, starts, period, width, members):
    step = panel_steps()[kind]
    for block, begin in enumerate(starts):
        span = slice(block * CHUNK, (block + 1) * CHUNK)
        out[:, span] = weight(cols[0:1, span], row_coord[...], step, begin, period, width, members)


def finish_kernel(row_coord, row_level, *refs, plan, period, width, members):
    out, scratch, sems = refs[-3], refs[-2], refs[-1]
    steps = panel_steps()
    coord, level = row_coord[...], row_level[...]
    copies = []
    at = 0
    for n, kind, starts in plan:
        cols, parts = refs[at], refs[at + 1 : at + 1 + n]
        at += 1 + n
        step = steps[kind]
        for block, begin in enumerate(starts):
            span = slice(block * CHUNK, (block + 1) * CHUNK)
            slot = len(copies)
            raw = parts[0][:, span]
            if len(parts) > 1:
                share = len(starts) // (len(parts) - 1)
                part = parts[1 + block // share]
                if part.dtype == jnp.int32:
                    raw = raw + unpack(part, block % share, raw.shape[0])
                else:
                    raw = raw + part[:, span]
            if cols.shape[0] == out.shape[0]:
                scale = cols[:, span]
            else:
                scale = weight(cols[0:1, span], coord, step, begin, period, width, members)
            c = scale * raw
            scratch[slot] = c - jnp.clip(c, -level, level)
            target = pl.multiple_of(step * width + begin, CHUNK)
            copy = pltpu.make_async_copy(scratch.at[slot], out.at[:, pl.ds(target, CHUNK)], sems.at[slot])
            copy.start()
            copies.append(copy)
    for copy in copies:
        copy.wait()


def finish(row_coord, row_level, groups, out, shape, period, width, members):
    operands = [row_coord, row_level]
    plan = []
    for cols, parts, kind, starts in groups:
        operands += [cols, *parts]
        plan.append((len(parts), kind, starts))
    copies = sum(len(starts) for _, _, starts in plan)
    specs = [VMEM] * len(operands)
    aliases = {}
    if out is not None:
        aliases = {len(operands): 0}
        operands.append(out)
        specs.append(pl.BlockSpec(memory_space=pl.ANY))
    return pl.pallas_call(
        functools.partial(finish_kernel, plan=plan, period=period, width=width, members=members),
        out_shape=jax.ShapeDtypeStruct(shape, F32),
        in_specs=specs,
        out_specs=pl.BlockSpec(memory_space=pl.ANY),
        scratch_shapes=[pltpu.VMEM((copies, shape[0], CHUNK), F32), pltpu.SemaphoreType.DMA((copies,))],
        input_output_aliases=aliases,
        compiler_params=PARAMS,
        cost_estimate=pl.CostEstimate(flops=1, bytes_accessed=1, transcendentals=0),
        name="finish",
    )(*operands)


def per_device(perturbations, node_coord, threshold_level):
    members, width = perturbations.shape
    groups = lax.axis_size("mem")
    count = lax.axis_size("mesh")
    period = 4.0 * width * count
    owned = width // groups
    everyone = members * groups
    split = groups == 2
    rows = [owned] * groups if split else [width]
    shape = (owned, 4 * width)
    coord = node_coord.reshape(1, width)
    levels = threshold_level.reshape(1, width)

    def permute(array, pairs):
        return lax.ppermute(array, "mesh", pairs)

    everywhere = range(count)
    swap_x = [(p, p ^ 2) for p in everywhere]
    relay = [(p, (p - 4) % count) for p in everywhere if p % 4 >= 2]
    back_two = [(p, (p - 2) % count) for p in everywhere]
    siblings = [(p, p ^ 1) for p in everywhere]
    extra_pairs = [(p, p - 1) if p % 2 else (p, (p - 3) % count) for p in everywhere]

    def reduced(parts):
        if split:
            return [parts[-1]] + [lax.ppermute(a, "mem", [(0, 1), (1, 0)]) for a in parts[:-1]]
        return [lax.psum_scatter(parts[0], "mem", scatter_dimension=0, tiled=True)]

    half = width // 2
    low = perturbations[:, :half]
    rest = after(perturbations, low)
    high, *highs = prepare(rest[:, half:], rest[members - TAIL :, :half], coord)
    lt, row_coord, row_level, *own = own_tile(low, high, coord, levels, owned, rows)
    own_parts = reduced(own)
    own_cols = jnp.concatenate([high[members : members + PAD // 2], high[members + PAD // 2 :]], axis=1).astype(F32)

    first = permute(head(low), swap_x)
    extra = [permute(a, extra_pairs) for a in (low, high)]
    straight = [permute(after(a, first), back_two) for a in highs]
    near = cut(first)
    passed = [permute(a, relay) for a in near]

    def tile(panels, picks, *tokens, keep=False):
        return panel_tile(after(lt, *tokens), panels, picks, rows, keep)

    def finished(out, token, *groups):
        groups = [(after(groups[0][0], token), *groups[0][1:])] + list(groups[1:])
        return finish(row_coord, row_level, groups, out, shape, period, width, everyone)

    extra_cols, *extra_parts = tile(extra, [[0, 1]], own_parts[-1])
    extra_parts = reduced(extra_parts)
    whole = [i * CHUNK for i in range(width // CHUNK)]
    places = [whole[::2], whole[1::2]]
    sides = [[0, 2], [1, 2]]
    cols0, *parts0, two0 = tile([near[0], passed[0], straight[0]], sides, extra_cols, keep=True)
    parts0 = reduced(parts0)
    out = finished(None, cols0, (own_cols, own_parts, "own", whole), (extra_cols, extra_parts, "extra", whole))
    cols1, *parts1, two1 = tile([near[1], passed[1], straight[1]], sides, out, parts0[-1], keep=True)
    parts1 = reduced(parts1)
    other0, other1 = permute(two0, siblings), permute(two1, siblings)
    other_cols0, *other_parts0 = tile([other0], [[0]], cols1)
    other_parts0 = reduced(other_parts0)
    other_cols1, *other_parts1 = tile([other1], [[0]], other_cols0)
    other_parts1 = reduced(other_parts1)
    weights = call(
        functools.partial(
            weigh_kernel, kind="other", starts=places[1], period=period, width=width, members=everyone
        ),
        [jax.ShapeDtypeStruct((owned, half), F32)],
        row_coord,
        other_cols1,
        name="weigh",
    )[0]
    out = finished(
        out,
        weights,
        (cols0, parts0, "two", places[0]),
        (cols1, parts1, "two", places[1]),
        (other_cols0, other_parts0, "other", places[0]),
    )
    return finished(out, other_cols1, (weights, other_parts1, "other", places[1]))


def solution(mesh):
    in_specs = (P("mem", "mesh"), P("mesh"), P("mesh"))
    out_specs = P(("mesh", "mem"), None)
    return jax.shard_map(
        per_device, mesh=mesh, in_specs=in_specs, out_specs=out_specs, check_vma=False
    )
```

```python
import functools

import jax
import jax.numpy as jnp
from jax import lax
from jax.experimental import pallas as pl
from jax.experimental.pallas import tpu as pltpu
from jax.sharding import PartitionSpec as P

PAD = 16
TAIL = 32
STEPS = 32766.0
CHUNK = 128
PARAMS = pltpu.CompilerParams(vmem_limit_bytes=32 * 1024 * 1024)
VMEM = pl.BlockSpec(memory_space=pltpu.VMEM)
F32 = jnp.float32


def after(value, *tokens):
    return lax.optimization_barrier((value, *tokens))[0]


def call(kernel, outs, *operands, name, flops=0):
    size = sum(o.size * o.dtype.itemsize for o in (*outs, *operands))
    return pl.pallas_call(
        kernel,
        out_shape=outs,
        in_specs=[VMEM] * len(operands),
        out_specs=[VMEM] * len(outs),
        compiler_params=PARAMS,
        cost_estimate=pl.CostEstimate(flops=1, bytes_accessed=1, transcendentals=0),
        name=name,
    )(*operands)


def gc_taper(r):
    near = 1.0 + r * r * (-5.0 / 3.0 + r * (0.625 + r * (0.5 - 0.25 * r)))
    s = jnp.maximum(r, 1.0)
    far = 4.0 - 5.0 * s + s * s * (5.0 / 3.0 + s * (0.625 + s * (s * (1.0 / 12.0) - 0.5))) - (2.0 / 3.0) / s
    return jnp.where(r <= 1.0, near, jnp.where(r <= 2.0, far, 0.0))


def prepare_kernel(x, coord, high, *parts):
    members, width = x.shape
    half = width // 2
    first = 4 * width * lax.axis_index("mesh")
    jitter = coord[...] - first - 4 * lax.broadcasted_iota(jnp.int32, (1, width), 1)
    jitter = jitter.astype(F32)
    high[:members, :] = x[:, half:]
    high[members:, :] = jnp.concatenate(
        [jnp.broadcast_to(jitter[:, :half], (PAD // 2, half)), jnp.broadcast_to(jitter[:, half:], (PAD // 2, half))],
        axis=0,
    ).astype(x.dtype)
    for i, part in enumerate(parts):
        span = slice(i * CHUNK, (i + 1) * CHUNK)
        part[: members + PAD, :] = high[:, span]
        part[members + PAD :, :] = x[members - TAIL :, span]


def cut_kernel(whole, *parts):
    wide = parts[0].shape[1]
    for i, part in enumerate(parts):
        part[...] = whole[:, i * wide : (i + 1) * wide]


def cut(panel):
    half = jax.ShapeDtypeStruct((panel.shape[0], panel.shape[1] // 2), panel.dtype)
    return call(cut_kernel, [half] * 2, panel, name="cut")


def head_kernel(whole, part):
    part[...] = whole[: part.shape[0], :]


def head(panel):
    short = jax.ShapeDtypeStruct((panel.shape[0] - TAIL, panel.shape[1]), panel.dtype)
    return call(head_kernel, [short], panel, name="head")[0]


def prepare(x, coord):
    members, width = x.shape
    outs = [jax.ShapeDtypeStruct((members + PAD, width // 2), x.dtype)]
    outs += [jax.ShapeDtypeStruct((members + PAD + TAIL, CHUNK), x.dtype)] * (width // 2 // CHUNK)
    return call(prepare_kernel, outs, x, coord, name="prepare")


def own_kernel(low, high, coord, level, lt, row_coord, row_level, *outs, owned, split):
    width, members = lt.shape
    groups = width // owned
    half = width // 2
    mem = lax.axis_index("mem")
    for at, part in ((0, low), (half, high)):
        columns = part[:members, :].T
        if split:
            begin = lax.rem(mem + 1 + at // half, 2) * half
            lt[pl.ds(pl.multiple_of(begin, half), half), :] = columns
        else:
            lt[at : at + half, :] = columns
    for at, part in ((0, low), (half, high)):
        tile = jnp.dot(lt[...], part[:members, :], preferred_element_type=F32)
        store_rows(tile, outs, at)
    rows = jnp.concatenate(
        [jnp.broadcast_to(coord[...], (CHUNK, width)), jnp.broadcast_to(level[...], (CHUNK, width))], axis=0
    )
    rows = rows.astype(F32)
    for part in range(groups):

        @pl.when(mem == part)
        def _():
            span = slice(part * owned, (part + 1) * owned)
            row_coord[...] = rows[:CHUNK, span].T
            row_level[...] = 0.05 * rows[CHUNK:, span].T


def store_rows(tile, outs, at):
    first = 0
    for out in outs:
        out[:, at : at + tile.shape[1]] = tile[first : first + out.shape[0]]
        first += out.shape[0]


def own_tile(low, high, coord, level, owned, rows):
    members, width = low.shape[0], 2 * low.shape[1]
    return call(
        functools.partial(own_kernel, owned=owned, split=len(rows) > 1),
        [jax.ShapeDtypeStruct((width, members), low.dtype)]
        + [jax.ShapeDtypeStruct((owned, CHUNK), F32)] * 2
        + [jax.ShapeDtypeStruct((r, width), F32) for r in rows],
        low,
        high,
        coord,
        level,
        name="own_tile",
        flops=2 * members * width * width,
    )


def narrowed(block):
    top = jnp.maximum(jnp.max(jnp.abs(block), axis=0, keepdims=True), 2.0**-126)
    power = jnp.ceil(8.0 * jnp.log2(top) + 0.01)
    root = jnp.exp2(-0.0625 * power)
    steps = jnp.round((block * root) * (root * STEPS))
    return steps.astype(jnp.int32), power.astype(jnp.int32)


def widened(steps, power):
    root = jnp.exp2(0.0625 * power.astype(F32))
    return (steps.astype(F32) * (root * (1.0 / STEPS))) * root


def pack(tile, packed):
    rows = tile.shape[0]
    for at in range(0, tile.shape[1] // 2, CHUNK):
        span = slice(at, at + CHUNK)
        high, high_power = narrowed(tile[:, 2 * at : 2 * at + CHUNK])
        low, low_power = narrowed(tile[:, 2 * at + CHUNK : 2 * at + 2 * CHUNK])
        packed[:rows, span] = (high << 16) | (low & 0xFFFF)
        packed[rows : rows + 4, span] = jnp.broadcast_to(high_power, (4, CHUNK))
        packed[rows + 4 :, span] = jnp.broadcast_to(low_power, (4, CHUNK))


def unpack(packed, block, rows):
    span = slice((block // 2) * CHUNK, (block // 2 + 1) * CHUNK)
    words = packed[:rows, span]
    if block % 2 == 0:
        return widened(words >> 16, packed[rows : rows + 1, span])
    return widened((words << 16) >> 16, packed[rows + 4 : rows + 5, span])


def panel_kernel(lt, *refs, picks, count, rows, keep):
    panels, cols, outs = refs[:count], refs[count], refs[count + 1 :]
    members = lt.shape[1]

    def run(which):
        chosen = [panels[i] for i in which]
        half = cols.shape[1] // 2
        pad = [chosen[-1][members : members + PAD, :].astype(F32)] * 2
        if len(chosen) == 1:
            pad = [pad[0][:, :half], pad[0][:, half:]]
        cols[:, :half] = pad[0][: PAD // 2]
        cols[:, half:] = pad[1][PAD // 2 :]
        blocks = [panel[:members, :] for panel in chosen]
        if chosen[0].shape[0] < members:
            blocks[0] = jnp.concatenate([chosen[0][...], chosen[1][members + PAD :, :]], axis=0)
        if keep:
            for at, block in zip((0, half), blocks):
                outs[-1][:members, at : at + half] = block
                outs[-1][members:, at : at + half] = chosen[-1][members : members + PAD, :]
        block = jnp.concatenate(blocks, axis=1)
        tile = jnp.dot(lt[...], block, preferred_element_type=F32)
        if len(rows) > 1:
            pack(tile[: rows[0]], outs[0])
            outs[1][...] = tile[rows[0] :]
        else:
            outs[0][...] = tile

    if len(picks) == 1:
        run(picks[0])
    else:
        cross = lax.rem(lax.axis_index("mesh") // 2, 2)
        for value, which in enumerate(picks):
            pl.when(cross == value)(functools.partial(run, which))


def panel_tile(lt, panels, picks, rows, keep=False):
    wide = sum(panels[i].shape[1] for i in picks[0])
    width, members = lt.shape
    return call(
        functools.partial(panel_kernel, picks=picks, count=len(panels), rows=rows, keep=keep),
        [jax.ShapeDtypeStruct((8, wide), F32)]
        + ([jax.ShapeDtypeStruct((rows[0] + 8, wide // 2), jnp.int32)] if len(rows) > 1 else [])
        + [jax.ShapeDtypeStruct((rows[-1], wide), F32)]
        + ([jax.ShapeDtypeStruct((members + PAD, wide), lt.dtype)] if keep else []),
        lt,
        *panels,
        name="panel_tile",
    )


def panel_steps():
    odd = lax.rem(lax.axis_index("mesh"), 2)
    return {"own": 0, "two": 2, "extra": 1 + 2 * odd, "other": 3 - 2 * odd}


def weight(offsets, row_coord, step, first, period, width, members):
    panel = lax.rem(lax.axis_index("mesh") + step, lax.axis_size("mesh"))
    base = (4 * (panel * width + first)).astype(F32)
    place = 4 * lax.broadcasted_iota(jnp.int32, (1, CHUNK), 1)
    gap = jnp.abs(offsets + (base + place.astype(F32)) - row_coord)
    dist = jnp.minimum(gap, period - gap)
    return gc_taper(dist * (1.0 / (12 * width))) * (1.0 / (members - 1))


def weigh_kernel(row_coord, cols, out, *, kind, starts, period, width, members):
    step = panel_steps()[kind]
    for block, begin in enumerate(starts):
        span = slice(block * CHUNK, (block + 1) * CHUNK)
        out[:, span] = weight(cols[0:1, span], row_coord[...], step, begin, period, width, members)


def finish_kernel(row_coord, row_level, *refs, plan, period, width, members):
    out, scratch, sems = refs[-3], refs[-2], refs[-1]
    steps = panel_steps()
    coord, level = row_coord[...], row_level[...]
    copies = []
    at = 0
    for n, kind, starts in plan:
        cols, parts = refs[at], refs[at + 1 : at + 1 + n]
        at += 1 + n
        step = steps[kind]
        for block, begin in enumerate(starts):
            span = slice(block * CHUNK, (block + 1) * CHUNK)
            slot = len(copies)
            raw = parts[0][:, span]
            if len(parts) > 1:
                share = len(starts) // (len(parts) - 1)
                part = parts[1 + block // share]
                if part.dtype == jnp.int32:
                    raw = raw + unpack(part, block % share, raw.shape[0])
                else:
                    raw = raw + part[:, span]
            if cols.shape[0] == out.shape[0]:
                scale = cols[:, span]
            else:
                scale = weight(cols[0:1, span], coord, step, begin, period, width, members)
            c = scale * raw
            scratch[slot] = c - jnp.clip(c, -level, level)
            target = pl.multiple_of(step * width + begin, CHUNK)
            copy = pltpu.make_async_copy(scratch.at[slot], out.at[:, pl.ds(target, CHUNK)], sems.at[slot])
            copy.start()
            copies.append(copy)
    for copy in copies:
        copy.wait()


def finish(row_coord, row_level, groups, out, shape, period, width, members):
    operands = [row_coord, row_level]
    plan = []
    for cols, parts, kind, starts in groups:
        operands += [cols, *parts]
        plan.append((len(parts), kind, starts))
    copies = sum(len(starts) for _, _, starts in plan)
    specs = [VMEM] * len(operands)
    aliases = {}
    if out is not None:
        aliases = {len(operands): 0}
        operands.append(out)
        specs.append(pl.BlockSpec(memory_space=pl.ANY))
    return pl.pallas_call(
        functools.partial(finish_kernel, plan=plan, period=period, width=width, members=members),
        out_shape=jax.ShapeDtypeStruct(shape, F32),
        in_specs=specs,
        out_specs=pl.BlockSpec(memory_space=pl.ANY),
        scratch_shapes=[pltpu.VMEM((copies, shape[0], CHUNK), F32), pltpu.SemaphoreType.DMA((copies,))],
        input_output_aliases=aliases,
        compiler_params=PARAMS,
        cost_estimate=pl.CostEstimate(flops=1, bytes_accessed=1, transcendentals=0),
        name="finish",
    )(*operands)


def per_device(perturbations, node_coord, threshold_level):
    members, width = perturbations.shape
    groups = lax.axis_size("mem")
    count = lax.axis_size("mesh")
    period = 4.0 * width * count
    owned = width // groups
    everyone = members * groups
    split = groups == 2
    rows = [owned] * groups if split else [width]
    shape = (owned, 4 * width)
    coord = node_coord.reshape(1, width)
    levels = threshold_level.reshape(1, width)

    def permute(array, pairs):
        return lax.ppermute(array, "mesh", pairs)

    everywhere = range(count)
    swap_x = [(p, p ^ 2) for p in everywhere]
    relay = [(p, (p - 4) % count) for p in everywhere if p % 4 >= 2]
    back_two = [(p, (p - 2) % count) for p in everywhere]
    siblings = [(p, p ^ 1) for p in everywhere]
    extra_pairs = [(p, p - 1) if p % 2 else (p, (p - 3) % count) for p in everywhere]

    def reduced(parts):
        if split:
            return [parts[-1]] + [lax.ppermute(a, "mem", [(0, 1), (1, 0)]) for a in parts[:-1]]
        return [lax.psum_scatter(parts[0], "mem", scatter_dimension=0, tiled=True)]

    half = width // 2
    low = perturbations[:, :half]
    high, *highs = prepare(after(perturbations, low), coord)
    lt, row_coord, row_level, *own = own_tile(low, high, coord, levels, owned, rows)
    own_parts = reduced(own)
    own_cols = jnp.concatenate([high[members : members + PAD // 2], high[members + PAD // 2 :]], axis=1).astype(F32)

    first = permute(head(low), swap_x)
    extra = [permute(a, extra_pairs) for a in (low, high)]
    straight = [permute(after(a, first), back_two) for a in highs]
    near = cut(first)
    passed = [permute(a, relay) for a in near]

    def tile(panels, picks, *tokens, keep=False):
        return panel_tile(after(lt, *tokens), panels, picks, rows, keep)

    def finished(out, token, *groups):
        groups = [(after(groups[0][0], token), *groups[0][1:])] + list(groups[1:])
        return finish(row_coord, row_level, groups, out, shape, period, width, everyone)

    extra_cols, *extra_parts = tile(extra, [[0, 1]], own_parts[-1])
    extra_parts = reduced(extra_parts)
    whole = [i * CHUNK for i in range(width // CHUNK)]
    places = [whole[::2], whole[1::2]]
    sides = [[0, 2], [1, 2]]
    cols0, *parts0, two0 = tile([near[0], passed[0], straight[0]], sides, extra_cols, keep=True)
    parts0 = reduced(parts0)
    out = finished(None, cols0, (own_cols, own_parts, "own", whole), (extra_cols, extra_parts, "extra", whole))
    cols1, *parts1, two1 = tile([near[1], passed[1], straight[1]], sides, out, parts0[-1], keep=True)
    parts1 = reduced(parts1)
    other0, other1 = permute(after(two0, out), siblings), permute(two1, siblings)
    other_cols0, *other_parts0 = tile([other0], [[0]], cols1)
    other_parts0 = reduced(other_parts0)
    other_cols1, *other_parts1 = tile([other1], [[0]], other_cols0)
    other_parts1 = reduced(other_parts1)
    weights = call(
        functools.partial(
            weigh_kernel, kind="other", starts=places[1], period=period, width=width, members=everyone
        ),
        [jax.ShapeDtypeStruct((owned, half), F32)],
        row_coord,
        other_cols1,
        name="weigh",
    )[0]
    out = finished(
        out,
        weights,
        (cols0, parts0, "two", places[0]),
        (cols1, parts1, "two", places[1]),
        (other_cols0, other_parts0, "other", places[0]),
    )
    return finished(out, other_cols1, (weights, other_parts1, "other", places[1]))


def solution(mesh):
    in_specs = (P("mem", "mesh"), P("mesh"), P("mesh"))
    out_specs = P(("mesh", "mem"), None)
    return jax.shard_map(
        per_device, mesh=mesh, in_specs=in_specs, out_specs=out_specs, check_vma=False
    )
```
